128 devices in a mesh: wide: 8 (over y, core), narrow: 16 (over x, z).
Axes of the slice: x: 4, y: 4, z: 4, core: 2. Of those that a mesh axis runs over, the one named last changes fastest.
Arguments:
- slip: bfloat16 [2, 524288], P(None, ('wide', 'narrow')), may hold values from -6 to 6
- effect_stress: float32 [2, 524288], P(None, ('wide', 'narrow')), may hold values from 0.5 to 4
- home_blocks: int32 [2048], P(('wide', 'narrow')), may hold values from 0 to 2047, as said below
- far_list: int32 [3, 49152], P(None, ('wide', 'narrow')), may hold values from 0 to 2047, as said below
- u_factor: bfloat16 [49152, 32, 256], P(('wide', 'narrow')), may hold values from -0.1875 to 0.1875
- v_factor: bfloat16 [49152, 32, 256], P(('wide', 'narrow')), may hold values from -0.1875 to 0.1875
- near_list: int32 [3, 8192], P(None, ('wide', 'narrow')), may hold values from 0 to 2047, as said below
- near_block: bfloat16 [8192, 256, 256], P(('wide', 'narrow')), may hold values from -0.1875 to 0.1875
Outputs:
- stress_first: float32 [2, 524288], P(None, ('wide', 'narrow'))
- stress_second: float32 [2, 524288], P(None, ('wide', 'narrow'))
The draws below stay inside these ranges and needn't reach their ends.
Inputs may be any that keep to these rules, and one draw needn't show every extreme that they name: `home_blocks`: a permutation of the 2048 blocks. `far_list`: entry e lies on device e // 384; its row block is one that this device stores (among its 16 positions of home_blocks); its column block may be any block. Among one device's entries at most 4 have column blocks stored by any one device, and on every device exactly 4 do for some storing device. The slots of one device are a permutation of 0 to 383. `near_list`: entry n lies on device n // 64; its row and column blocks are both stored by that device. The slots of one device are a permutation of 0 to 63.
All inputs are finite; a program needn't handle non-finite values.
Results may differ from the reference program's by a relative error of at most 0.0034.
Values may be sent and summed in bfloat16 or wider, within the bound.
A program may use at most 128 MiB of HBM per device.

```python
import math
import jax
import jax.numpy as jnp
from jax import lax

B = 256
R = 32
NB_DEV = 16
NEAR_ROW = 4
ADM_DEV = 384
NEAR_DEV = 64
CAP = 4
NBLK = 2048
NPATCH = 524288
NADM = 49152
NNEAR = 8192
N_WIDE = 8
N_NARROW = 16


def shared_layout(key):
    return jax.random.permutation(key, NBLK).astype(jnp.int32)


def draw_home_blocks(key, part):
    home_order = shared_layout(key)
    return home_order


def draw_far_list(key, part):
    home_order = shared_layout(key)
    key = jax.random.fold_in(key, 2)
    device_count = NBLK // NB_DEV

    def one_device(device_key, device):
        keys = jax.random.split(device_key, 6)
        favored = jax.random.randint(keys[0], (), 0, device_count)
        pool_owner = jnp.arange(device_count * CAP, dtype=jnp.int32) // CAP
        scores = jax.random.permutation(keys[1], device_count * CAP).astype(jnp.int32)
        scores = jnp.where(pool_owner == favored, scores - device_count * CAP, scores)
        chosen = pool_owner[jnp.argsort(scores)[:ADM_DEV]]
        chosen = chosen[jax.random.permutation(keys[2], ADM_DEV)]
        col_slot = jax.random.randint(keys[3], (ADM_DEV,), 0, NB_DEV)
        row_slot = jax.random.randint(keys[4], (ADM_DEV,), 0, NB_DEV)
        slot_order = jax.random.permutation(keys[5], ADM_DEV).astype(jnp.int32)
        row_blocks = home_order[device * NB_DEV + row_slot]
        col_blocks = home_order[chosen * NB_DEV + col_slot]
        return jnp.stack([row_blocks, col_blocks, slot_order])
    listed = jax.vmap(one_device)(jax.random.split(key, device_count), jnp.arange(device_count, dtype=jnp.int32))
    return listed.transpose(1, 0, 2).reshape(3, device_count * ADM_DEV).astype(jnp.int32)


def draw_near_list(key, part):
    home_order = shared_layout(key)
    key = jax.random.fold_in(key, 3)
    device_count = NBLK // NB_DEV

    def one_device(device_key, device):
        keys = jax.random.split(device_key, 3)
        row_slot = jax.random.randint(keys[0], (NEAR_DEV,), 0, NB_DEV)
        col_slot = jax.random.randint(keys[1], (NEAR_DEV,), 0, NB_DEV)
        slot_order = jax.random.permutation(keys[2], NEAR_DEV).astype(jnp.int32)
        return jnp.stack([home_order[device * NB_DEV + row_slot], home_order[device * NB_DEV + col_slot], slot_order])
    listed = jax.vmap(one_device)(jax.random.split(key, device_count), jnp.arange(device_count, dtype=jnp.int32))
    return listed.transpose(1, 0, 2).reshape(3, device_count * NEAR_DEV).astype(jnp.int32)


def levels(stream_key, dims, shards, least, top_value):
    factor_of = 1.0
    for dim, parts in shards:
        heights = jax.random.uniform(jax.random.fold_in(jax.random.fold_in(stream_key, 6), dim), (parts,), jnp.float32, least / len(shards), top_value / len(shards))
        factor_of = factor_of * jnp.repeat(jnp.exp(heights), dims[dim] // parts).reshape((-1,) + (1,) * (len(dims) - 1 - dim))
    return factor_of


def noise(rng, extent, deviation, reach, cuts=(), kind=jnp.bfloat16):
    result = jax.random.normal(rng, extent, jnp.float32) * deviation
    if len(cuts) > 0:
        result = levels(rng, extent, cuts, -0.22, 0.18) * result
    return jnp.clip(result, min=-reach, max=reach).astype(kind)


def setup_inputs(seed: int = 0) -> dict:
    splits = jax.random.split(jax.random.key(seed), 9)
    return {
        "slip": noise(splits[0], (2, NPATCH), 1.0, 6.0, ((1, 128),)),
        "effect_stress": jnp.clip(jnp.exp(math.log(4.0) - 2.0794415 * jax.random.uniform(splits[1], (2, NPATCH), jnp.float32) ** levels(splits[1], (2, NPATCH), ((1, 128),), -0.2, 0.2)), 0.5, 4.0),
        "home_blocks": draw_home_blocks(jax.random.fold_in(splits[8], 71), 0),
        "far_list": draw_far_list(jax.random.fold_in(splits[8], 71), 0),
        "u_factor": noise(splits[4], (NADM, R, B), (4 * B) ** -0.5, 0.1875, ((0, 128),)),
        "v_factor": noise(splits[5], (NADM, R, B), (4 * B) ** -0.5, 0.1875, ((0, 128),)),
        "near_list": draw_near_list(jax.random.fold_in(splits[8], 71), 0),
        "near_block": noise(splits[7], (NNEAR, B, B), (NEAR_ROW * B) ** -0.5, 0.1875, ((0, 128),)),
    }


def apply_kernel(rates, home_blocks, far_list, u_factor, v_factor, near_list, near_block):
    block_count = NB_DEV * N_WIDE * N_NARROW
    device_count = N_WIDE * N_NARROW
    position = jnp.zeros((block_count,), jnp.int32).at[home_blocks].set(jnp.arange(block_count, dtype=jnp.int32))
    blocks = rates.reshape(2, block_count, B).transpose(1, 0, 2).astype(jnp.float32)
    highest = lax.Precision.HIGHEST

    def far_step(device, accumulated):
        begin = (device * ADM_DEV).astype(jnp.int32)
        entry_lists = lax.dynamic_slice_in_dim(far_list, begin, ADM_DEV, 1)
        u_dev = lax.dynamic_slice_in_dim(u_factor, begin, ADM_DEV, 0)[entry_lists[2]].astype(jnp.float32)
        v_dev = lax.dynamic_slice_in_dim(v_factor, begin, ADM_DEV, 0)[entry_lists[2]].astype(jnp.float32)
        row_places = position[entry_lists[0]]
        col_places = position[entry_lists[1]]
        reduced = jnp.einsum('erb,ecb->ecr', v_dev, blocks[col_places], precision=highest)
        reduced = lax.optimization_barrier(reduced.astype(jnp.bfloat16)).astype(jnp.float32)
        forward_terms = jnp.einsum('erb,ecr->ecb', u_dev, reduced, precision=highest)
        projected = jnp.einsum('erb,ecb->ecr', u_dev, blocks[row_places], precision=highest)
        projected = lax.optimization_barrier(projected.astype(jnp.bfloat16)).astype(jnp.float32)
        back_terms = jnp.einsum('erb,ecr->ecb', v_dev, projected, precision=highest)
        return accumulated.at[row_places].add(forward_terms).at[col_places].add(back_terms)

    def near_step(device, accumulated):
        begin = (device * NEAR_DEV).astype(jnp.int32)
        entry_lists = lax.dynamic_slice_in_dim(near_list, begin, NEAR_DEV, 1)
        dense = lax.dynamic_slice_in_dim(near_block, begin, NEAR_DEV, 0)[entry_lists[2]].astype(jnp.float32)
        row_places = position[entry_lists[0]]
        col_places = position[entry_lists[1]]
        near_terms = jnp.einsum('nij,ncj->nci', dense, blocks[col_places], precision=highest)
        return accumulated.at[row_places].add(near_terms)

    accumulated = jnp.zeros((block_count, 2, B), jnp.float32)
    accumulated = lax.fori_loop(0, device_count, far_step, accumulated)
    accumulated = lax.fori_loop(0, device_count, near_step, accumulated)
    return accumulated.transpose(1, 0, 2).reshape(2, block_count * B)


def reference(slip, effect_stress, home_blocks, far_list, u_factor, v_factor, near_list, near_block):
    stress_first = apply_kernel(slip, home_blocks, far_list, u_factor, v_factor, near_list, near_block)
    mid_rate = (slip.astype(jnp.float32) * jnp.exp(jnp.tanh(stress_first / effect_stress))).astype(jnp.bfloat16)
    stress_second = apply_kernel(mid_rate, home_blocks, far_list, u_factor, v_factor, near_list, near_block)
    return (stress_first, stress_second)
```

```python
import functools

import jax
import jax.numpy as jnp
from jax import lax
from jax.experimental import pallas as pl
from jax.experimental.pallas import tpu as pltpu
from jax.sharding import PartitionSpec as P

AXES = ("wide", "narrow")
MESH = pl.DeviceIdType.MESH
BF = jnp.bfloat16
F32 = jnp.float32
I32 = jnp.int32
STRIDE = 37


def dot_nt(a, b):
    return lax.dot_general(a, b, (((1,), (1,)), ((), ())), preferred_element_type=F32)


def dot_nn(a, b):
    return lax.dot_general(a, b, (((1,), (0,)), ((), ())), preferred_element_type=F32)


def hot(mask):
    return jnp.where(mask, 1.0, 0.0).astype(BF)


def iota(shape, dim):
    return lax.broadcasted_iota(I32, shape, dim)


def rows_at(start, size):
    return pl.ds(pl.multiple_of(start, size), size)


def kernel(
    dims,
    home, far, near_list, x_in, effect, u_hbm, v_hbm, near_hbm,
    first_out, second_out,
    u, v, near, index, pair_hot, slot_val, order, tri, slot_hot, row_sel, row_sel_t,
    near_place, near_cols, near_left, col_sel, col_sel_t, reply_sel, reply_sel_t, rep,
    left, mid, terms, terms_low, flat,
    sent, got,
    load_sem, gather_send, gather_recv, send_sem, recv_sem,
):
    wide_n, narrow_n, nb, cap, adm, near_n, block, rank = dims
    devices = wide_n * narrow_n
    tiles = adm // 8
    cols2 = 2 * adm
    per = 2 * cap
    index_rows = index.shape[1] - 1
    half = block // 2
    my_wide = lax.axis_index("wide")
    my_narrow = lax.axis_index("narrow")
    me = my_wide * narrow_n + my_narrow

    loads = [
        pltpu.make_async_copy(u_hbm, u, load_sem.at[0]),
        pltpu.make_async_copy(v_hbm, v, load_sem.at[1]),
        pltpu.make_async_copy(near_hbm, near, load_sem.at[2]),
    ]
    for load in loads:
        load.start()

    def narrow_peer(j):
        return (my_wide, lax.rem(my_narrow + j, narrow_n))

    def wide_peer(j):
        return (lax.rem(my_wide + j, wide_n), my_narrow)

    barrier = pltpu.get_barrier_semaphore()
    for j in range(1, narrow_n):
        pl.semaphore_signal(barrier, inc=1, device_id=narrow_peer(j), device_id_type=MESH)
    for j in range(1, wide_n):
        pl.semaphore_signal(barrier, inc=1, device_id=wide_peer(j), device_id_type=MESH)

    far_cols = far[1:2, :]
    for r in range(index_rows):
        width = min(128, adm - r * 128)
        piece = far_cols[:, r * 128 : r * 128 + width]
        if width < 128:
            piece = jnp.concatenate([piece, jnp.full((1, 128 - width), -1, I32)], axis=1)
        index[me, r : r + 1, :] = piece
    lane = iota((1, 128), 1)
    home_row = jnp.full((1, 128), -1, I32)
    for s in range(nb):
        home_row = jnp.where(lane == s, home[s], home_row)
    index[me, index_rows : index_rows + 1, :] = home_row

    pl.semaphore_wait(barrier, narrow_n + wide_n - 2)

    for j in range(1, narrow_n):
        pltpu.make_async_remote_copy(
            src_ref=index.at[me], dst_ref=index.at[me],
            send_sem=gather_send.at[0], recv_sem=gather_recv.at[0],
            device_id=narrow_peer(j), device_id_type=MESH,
        ).start()

    row_slot = jnp.zeros((1, adm), I32)
    near_row = jnp.zeros((1, near_n), I32)
    near_col = jnp.zeros((1, near_n), I32)
    far_rows = far[0:1, :]
    for s in range(nb):
        row_slot = jnp.where(far_rows == home[s], s, row_slot)
        near_row = jnp.where(near_list[0:1, :] == home[s], s, near_row)
        near_col = jnp.where(near_list[1:2, :] == home[s], s, near_col)
    place = iota((cols2, adm), 0)
    slot_hot[...] = hot(lax.div(place, 16) * 8 + lax.rem(place, 8) == far[2:3, :])
    row_hot = hot(row_slot == lax.rem(iota((2 * nb, adm), 0), nb))
    pick = dot_nt(slot_hot[...], row_hot)
    comp = lax.rem(lax.div(iota((cols2, 2 * nb), 0), 8), 2)
    row_sel[...] = jnp.where(comp == lax.div(iota((cols2, 2 * nb), 1), nb), pick, 0.0).astype(BF)
    pick_t = dot_nt(row_hot, slot_hot[...])
    comp_t = lax.rem(lax.div(iota((2 * nb, cols2), 1), 8), 2)
    row_sel_t[...] = jnp.where(comp_t == lax.div(iota((2 * nb, cols2), 0), nb), pick_t, 0.0).astype(BF)
    tri[...] = hot(iota((adm, adm), 0) < iota((adm, adm), 1))

    near_key = near_list[2:3, :] * nb + near_row
    near_key2 = jnp.concatenate([near_key, near_key], axis=1)
    near_col2 = jnp.concatenate([near_col, near_col], axis=1)
    near_rows = near_n * 2 * nb
    where_row = iota((near_rows, 2 * near_n), 0)
    row_key = lax.div(where_row, 2 * nb) * nb + lax.rem(where_row, nb)
    row_comp = lax.rem(lax.div(where_row, nb), 2)
    lane_comp = lax.div(iota((near_rows, 2 * near_n), 1), near_n)
    near_place[...] = hot((row_key == near_key2) & (row_comp == lane_comp))
    col_row = iota((2 * nb, 2 * near_n), 0)
    col_mask = (near_col2 == lax.rem(col_row, nb)) & (
        lax.div(col_row, nb) == lax.div(iota((2 * nb, 2 * near_n), 1), near_n)
    )
    near_cols[...] = jnp.where(col_mask, 1.0, 0.0).T.astype(BF)

    chunk = 2 * per
    rep_rows = devices * per
    rep[...] = hot(lax.div(iota((rep_rows, devices), 0), per) == iota((rep_rows, devices), 1))

    def wait_bytes(ref, sem):
        pltpu.make_async_copy(ref, ref, sem).wait()

    wait_bytes(index.at[pl.ds(0, narrow_n - 1)], gather_recv.at[0])
    row_group = index.at[pl.ds(my_wide * narrow_n, narrow_n)]
    for j in range(1, wide_n):
        pltpu.make_async_remote_copy(
            src_ref=row_group, dst_ref=row_group,
            send_sem=gather_send.at[1], recv_sem=gather_recv.at[1],
            device_id=wide_peer(j), device_id_type=MESH,
        ).start()

    diag = lax.rem(iota((16, 8 * rank), 0), 8) == lax.div(iota((16, 8 * rank), 1), rank)
    unroll = 8 if tiles % 8 == 0 else 1

    def over_tiles(step):
        def body(i, carry):
            for k in range(unroll):
                step(i * unroll + k)
            return carry

        lax.fori_loop(0, tiles // unroll, body, 0)

    def contract(factor):
        def step(t):
            y = dot_nt(left[rows_at(t * 16, 16), :], factor[rows_at(t * 8 * rank, 8 * rank), :])
            mid[rows_at(t * 16, 16), :] = jnp.where(diag, y, 0.0).astype(BF)

        over_tiles(step)

    def expand(factor, split):
        def step(t):
            y = dot_nn(mid[rows_at(t * 16, 16), :], factor[rows_at(t * 8 * rank, 8 * rank), :])
            high = y.astype(BF)
            terms[rows_at(t * 16, 16), :] = high
            if split:
                terms_low[rows_at(t * 16, 16), :] = (y - high.astype(F32)).astype(BF)

        over_tiles(step)

    def send_all(n):
        def body(j, carry):
            to = lax.rem(me + j * STRIDE, devices)
            pltpu.make_async_remote_copy(
                src_ref=sent.at[n, to], dst_ref=got.at[n, me],
                send_sem=send_sem.at[n], recv_sem=recv_sem.at[n],
                device_id=(lax.div(to, narrow_n), lax.rem(to, narrow_n)), device_id_type=MESH,
            ).start()
            return carry

        lax.fori_loop(1, devices, body, 0)
        got[n, me] = sent[n, me]

    def stage(n, sel, right):
        parts = max(1, rep_rows // 256)
        size = rep_rows // parts

        def body(i, carry):
            y = dot_nn(sel[rows_at(i * size, size), :], right)
            y = y.reshape(size // per, per, block)
            y = jnp.concatenate([y[:, :, :half], y[:, :, half:]], axis=1)
            sent[n, rows_at(i * (size // per), size // per)] = y.astype(BF)
            return carry

        lax.fori_loop(0, parts, body, 0)

    def land(n):
        wait_bytes(got.at[n, pl.ds(0, devices - 1)], recv_sem.at[n])
        y = got[n].astype(F32)
        y = jnp.concatenate([y[:, :per, :], y[:, per:, :]], axis=2)
        flat[...] = y.reshape(rep_rows, block).astype(BF)

    def send_rates(n, x):
        stage(n, reply_sel, jnp.concatenate([x] * cap, axis=0))
        send_all(n)

    def near_part(x):
        near_x = dot_nn(near_cols[...], x).astype(BF)
        parts = max(1, near_rows // 256)
        size = near_rows // parts

        def place_body(i, carry):
            near_left[rows_at(i * size, size), :] = dot_nn(
                near_place[rows_at(i * size, size), :], near_x
            ).astype(BF)
            return carry

        lax.fori_loop(0, parts, place_body, 0)
        steps = 4

        def body(i, acc):
            for k in range(steps):
                g = i * steps + k
                acc = acc + dot_nt(
                    near_left[rows_at(g * 2 * nb, 2 * nb), :], near[rows_at(g * block, block), :]
                )
            return acc

        return lax.fori_loop(0, near_n // steps, body, jnp.zeros((2 * nb, block), F32))

    def row_rates(x):
        left[...] = dot_nn(row_sel[...], x).astype(BF)

    def send_back(n):
        stage(n, col_sel_t, terms[...])
        send_all(n)

    def finish(n_rates, n_back, total):
        land(n_rates)
        left[...] = dot_nn(col_sel[...], flat[...]).astype(BF)
        contract(v)
        expand(u, True)
        total = total + dot_nn(row_sel_t[...], terms[...])
        total = total + dot_nn(row_sel_t[...], terms_low[...])
        land(n_back)
        return total + dot_nn(reply_sel_t[...], flat[...])

    x = x_in[...]
    row_rates(x)
    loads[0].wait()
    contract(u)

    wait_bytes(index.at[pl.ds(0, (wide_n - 1) * narrow_n)], gather_recv.at[1])
    part = min(32, devices)
    for q in range(0, devices, part):
        wanted = jnp.concatenate(
            [index[q : q + part, r, :] for r in range(index_rows)], axis=1
        )[:, :adm]
        val = jnp.zeros((part, adm), F32)
        homes = index[q : q + part, index_rows, :]
        found = jnp.zeros((part, adm), F32)
        for s in range(nb):
            val = jnp.where(wanted == home[s], float(s + 1), val)
            found = jnp.where(homes[:, s : s + 1] == far_cols, 1.0, found)
        slot_val[q : q + part, :] = val
        pair_hot[q : q + part, :] = hot(val > 0.0)
        pair_hot[devices + q : devices + q + part, :] = found.astype(BF)
    order[...] = dot_nn(pair_hot[...], tri[...])
    lane_k = lax.div(iota((devices, 2 * nb * cap), 1), 2 * nb)
    lane_s = lax.rem(iota((devices, 2 * nb * cap), 1), nb) + 1
    chosen = jnp.zeros((devices, 2 * nb * cap), F32)
    for k in range(cap):
        slot_k = jnp.sum(
            jnp.where(order[:devices, :] == float(k), slot_val[...], 0.0), axis=1, keepdims=True
        )
        chosen = jnp.where(lane_k == k, slot_k, chosen)
    asked = jnp.where(chosen == lane_s.astype(F32), 1.0, 0.0)
    lanes = 2 * nb * cap
    reply_row = lax.rem(iota((rep_rows, lanes), 0), per)
    reply_mask = reply_row == lax.div(iota((rep_rows, lanes), 1), nb)
    reply_sel[...] = jnp.where(reply_mask, dot_nn(rep[...], asked.astype(BF)), 0.0).astype(BF)
    send_rates(0, x)

    reply_col = lax.rem(iota((lanes, rep_rows), 1), per)
    back_mask = reply_col == lax.div(iota((lanes, rep_rows), 0), nb)
    back_sel = jnp.where(back_mask, dot_nt(asked.T.astype(BF), rep[...]), 0.0)
    summed = back_sel[: 2 * nb]
    for k in range(1, cap):
        summed = summed + back_sel[2 * nb * k : 2 * nb * (k + 1)]
    reply_sel_t[...] = summed.astype(BF)

    found = pair_hot[devices:, :].astype(F32)
    owner = jnp.sum(found * iota((devices, adm), 0).astype(F32), axis=0, keepdims=True)
    place_in = jnp.sum(found * order[devices:, :], axis=0, keepdims=True)
    both = jnp.concatenate([owner, place_in, jnp.zeros((6, adm), F32)], axis=0).astype(BF)
    to_row = dot_nt(both, slot_hot[...])
    to_row = (to_row[0:1] * per + to_row[1:2] * 2).astype(I32)
    to_row = to_row + lax.rem(lax.div(iota((1, cols2), 1), 8), 2)
    col_sel_t[...] = hot(iota((rep_rows, cols2), 0) == to_row)
    to_col = dot_nt(slot_hot[...], both)
    to_col = (to_col[:, 0:1] * per + to_col[:, 1:2] * 2).astype(I32)
    to_col = to_col + lax.rem(lax.div(iota((cols2, 1), 0), 8), 2)
    col_sel[...] = hot(iota((cols2, rep_rows), 1) == to_col)

    loads[1].wait()
    expand(v, False)
    send_back(1)
    loads[2].wait()
    first = finish(0, 1, near_part(x))
    first_out[...] = first

    x = (x.astype(F32) * jnp.exp(jnp.tanh(first / effect[...]))).astype(BF)
    send_rates(2, x)
    row_rates(x)
    contract(u)
    expand(v, False)
    send_back(3)
    second_out[...] = finish(2, 3, near_part(x))

    wait_bytes(index.at[pl.ds(0, narrow_n - 1)], gather_send.at[0])
    wait_bytes(index.at[pl.ds(0, (wide_n - 1) * narrow_n)], gather_send.at[1])
    for n in range(4):
        wait_bytes(sent.at[n, pl.ds(0, devices - 1)], send_sem.at[n])


def local(slip, effect_stress, home_blocks, far_list, u_factor, v_factor, near_list, near_block):
    wide_n, narrow_n = lax.axis_size("wide"), lax.axis_size("narrow")
    devices = wide_n * narrow_n
    nb = home_blocks.shape[0]
    block = slip.shape[1] // nb
    adm, rank, _ = u_factor.shape
    near_n = near_list.shape[1]
    cap = max(2, adm // devices + 1)
    per = 2 * cap
    rep_rows = devices * per
    cols2 = 2 * adm
    index_rows = -(-adm // 128)
    dims = (wide_n, narrow_n, nb, cap, adm, near_n, block, rank)
    vmem = pl.BlockSpec(memory_space=pltpu.VMEM)
    smem = pl.BlockSpec(memory_space=pltpu.SMEM)
    hbm = pl.BlockSpec(memory_space=pl.ANY)
    field = jax.ShapeDtypeStruct((2 * nb, block), F32)
    dma = pltpu.SemaphoreType.DMA
    first, second = pl.pallas_call(
        functools.partial(kernel, dims),
        out_shape=(field, field),
        in_specs=[smem, vmem, vmem, vmem, vmem, hbm, hbm, hbm],
        out_specs=(vmem, vmem),
        scratch_shapes=[
            pltpu.VMEM((adm * rank, block), BF),
            pltpu.VMEM((adm * rank, block), BF),
            pltpu.VMEM((near_n * block, block), BF),
            pltpu.VMEM((devices, index_rows + 1, 128), I32),
            pltpu.VMEM((2 * devices, adm), BF),
            pltpu.VMEM((devices, adm), F32),
            pltpu.VMEM((2 * devices, adm), F32),
            pltpu.VMEM((adm, adm), BF),
            pltpu.VMEM((cols2, adm), BF),
            pltpu.VMEM((cols2, 2 * nb), BF),
            pltpu.VMEM((2 * nb, cols2), BF),
            pltpu.VMEM((near_n * 2 * nb, 2 * near_n), BF),
            pltpu.VMEM((2 * near_n, 2 * nb), BF),
            pltpu.VMEM((near_n * 2 * nb, block), BF),
            pltpu.VMEM((cols2, rep_rows), BF),
            pltpu.VMEM((rep_rows, cols2), BF),
            pltpu.VMEM((rep_rows, 2 * nb * cap), BF),
            pltpu.VMEM((2 * nb, rep_rows), BF),
            pltpu.VMEM((rep_rows, devices), BF),
            pltpu.VMEM((cols2, block), BF),
            pltpu.VMEM((cols2, 8 * rank), BF),
            pltpu.VMEM((cols2, block), BF),
            pltpu.VMEM((cols2, block), BF),
            pltpu.VMEM((rep_rows, block), BF),
            pltpu.VMEM((4, devices, 2 * per, block // 2), BF),
            pltpu.VMEM((4, devices, 2 * per, block // 2), BF),
            dma((3,)),
            dma((2,)),
            dma((2,)),
            dma((4,)),
            dma((4,)),
        ],
        compiler_params=pltpu.CompilerParams(
            collective_id=0, has_side_effects=True, vmem_limit_bytes=56 << 20
        ),
        name="stress_two_steps",
    )(
        home_blocks,
        far_list,
        near_list,
        slip.reshape(2 * nb, block),
        effect_stress.reshape(2 * nb, block),
        u_factor.reshape(adm * rank, block),
        v_factor.reshape(adm * rank, block),
        near_block.reshape(near_n * block, block),
    )
    return first.reshape(2, nb * block), second.reshape(2, nb * block)


def solution(mesh):
    in_specs = (
        P(None, AXES),
        P(None, AXES),
        P(AXES),
        P(None, AXES),
        P(AXES, None, None),
        P(AXES, None, None),
        P(None, AXES),
        P(AXES, None, None),
    )
    out_specs = (P(None, AXES), P(None, AXES))
    return jax.shard_map(local, mesh=mesh, in_specs=in_specs, out_specs=out_specs, check_vma=False)
```

```python
import functools
import itertools

import jax
import jax.numpy as jnp
from jax import lax
from jax.experimental import pallas as pl
from jax.experimental.pallas import tpu as pltpu
from jax.sharding import PartitionSpec as P

AXES = ("wide", "narrow")
MESH = pl.DeviceIdType.MESH
BF = jnp.bfloat16
F32 = jnp.float32
I32 = jnp.int32


def dot_nt(a, b):
    return lax.dot_general(a, b, (((1,), (1,)), ((), ())), preferred_element_type=F32)


def dot_nn(a, b):
    return lax.dot_general(a, b, (((1,), (0,)), ((), ())), preferred_element_type=F32)


def hot(mask):
    return jnp.where(mask, 1.0, 0.0).astype(BF)


def iota(shape, dim):
    return lax.broadcasted_iota(I32, shape, dim)


def far_first(extents):
    def hops(shift):
        return sum(min(d, n - d) for d, n, core in zip(shift, extents, (0, 1, 0, 0)) if not core)

    shifts = [s for s in itertools.product(*map(range, extents)) if any(s)]
    return sorted(shifts, key=hops, reverse=True)


def rows_at(start, size):
    return pl.ds(pl.multiple_of(start, size), size)


def kernel(
    dims,
    home, far, near_list, slip, effect, u_hbm, v_hbm, near_hbm,
    first_out, second_out,
    u, v, near, index, pair_hot, slot_val, order, tri, slot_hot, row_sel, row_sel_t,
    near_place, near_cols, near_left, col_sel, col_sel_t, reply_sel, reply_sel_t, rep,
    left, mid, terms, terms_low, flat,
    sent, got, field,
    load_sem, gather_send, gather_recv, send_sem, recv_sem,
):
    wide_n, narrow_n, nb, cap, adm, near_n, block, rank = dims
    devices = wide_n * narrow_n
    tiles = adm // 8
    cols2 = 2 * adm
    per = 2 * cap
    index_rows = index.shape[1] - 1
    half = block // 2
    my_wide = lax.axis_index("wide")
    my_narrow = lax.axis_index("narrow")
    me = my_wide * narrow_n + my_narrow

    loads = [
        pltpu.make_async_copy(u_hbm, u, load_sem.at[0]),
        pltpu.make_async_copy(v_hbm, v, load_sem.at[1]),
        pltpu.make_async_copy(near_hbm, near, load_sem.at[2]),
    ]
    for load in loads:
        load.start()

    def narrow_peer(j):
        return (my_wide, lax.rem(my_narrow + j, narrow_n))

    def wide_peer(j):
        return (lax.rem(my_wide + j, wide_n), my_narrow)

    barrier = pltpu.get_barrier_semaphore()
    for j in range(1, narrow_n):
        pl.semaphore_signal(barrier, inc=1, device_id=narrow_peer(j), device_id_type=MESH)
    for j in range(1, wide_n):
        pl.semaphore_signal(barrier, inc=1, device_id=wide_peer(j), device_id_type=MESH)

    far_cols = far[1:2, :]
    for r in range(index_rows):
        width = min(128, adm - r * 128)
        piece = far_cols[:, r * 128 : r * 128 + width]
        if width < 128:
            piece = jnp.concatenate([piece, jnp.full((1, 128 - width), -1, I32)], axis=1)
        index[me, r : r + 1, :] = piece
    lane = iota((1, 128), 1)
    home_row = jnp.full((1, 128), -1, I32)
    for s in range(nb):
        home_row = jnp.where(lane == s, home[s], home_row)
    index[me, index_rows : index_rows + 1, :] = home_row

    pl.semaphore_wait(barrier, narrow_n + wide_n - 2)

    for j in range(1, narrow_n):
        pltpu.make_async_remote_copy(
            src_ref=index.at[me], dst_ref=index.at[me],
            send_sem=gather_send.at[0], recv_sem=gather_recv.at[0],
            device_id=narrow_peer(j), device_id_type=MESH,
        ).start()

    row_slot = jnp.zeros((1, adm), I32)
    near_row = jnp.zeros((1, near_n), I32)
    near_col = jnp.zeros((1, near_n), I32)
    far_rows = far[0:1, :]
    for s in range(nb):
        row_slot = jnp.where(far_rows == home[s], s, row_slot)
        near_row = jnp.where(near_list[0:1, :] == home[s], s, near_row)
        near_col = jnp.where(near_list[1:2, :] == home[s], s, near_col)
    place = iota((cols2, adm), 0)
    slot_hot[...] = hot(lax.div(place, 16) * 8 + lax.rem(place, 8) == far[2:3, :])
    row_hot = hot(row_slot == lax.rem(iota((2 * nb, adm), 0), nb))
    pick = dot_nt(slot_hot[...], row_hot)
    comp = lax.rem(lax.div(iota((cols2, 2 * nb), 0), 8), 2)
    row_sel[...] = jnp.where(comp == lax.div(iota((cols2, 2 * nb), 1), nb), pick, 0.0).astype(BF)
    pick_t = dot_nt(row_hot, slot_hot[...])
    comp_t = lax.rem(lax.div(iota((2 * nb, cols2), 1), 8), 2)
    row_sel_t[...] = jnp.where(comp_t == lax.div(iota((2 * nb, cols2), 0), nb), pick_t, 0.0).astype(BF)
    tri[...] = hot(iota((adm, adm), 0) < iota((adm, adm), 1))

    near_key = near_list[2:3, :] * nb + near_row
    near_key2 = jnp.concatenate([near_key, near_key], axis=1)
    near_col2 = jnp.concatenate([near_col, near_col], axis=1)
    near_rows = near_n * 2 * nb
    where_row = iota((near_rows, 2 * near_n), 0)
    row_key = lax.div(where_row, 2 * nb) * nb + lax.rem(where_row, nb)
    row_comp = lax.rem(lax.div(where_row, nb), 2)
    lane_comp = lax.div(iota((near_rows, 2 * near_n), 1), near_n)
    near_place[...] = hot((row_key == near_key2) & (row_comp == lane_comp))
    col_row = iota((2 * nb, 2 * near_n), 0)
    col_mask = (near_col2 == lax.rem(col_row, nb)) & (
        lax.div(col_row, nb) == lax.div(iota((2 * nb, 2 * near_n), 1), near_n)
    )
    near_cols[...] = jnp.where(col_mask, 1.0, 0.0).T.astype(BF)

    chunk = 2 * per
    rep_rows = devices * per
    rep[...] = hot(lax.div(iota((rep_rows, devices), 0), per) == iota((rep_rows, devices), 1))

    def by_block(ref):
        for c in range(2):
            for s in range(nb):
                piece = ref[c : c + 1, s * block : (s + 1) * block]
                field[c * nb + s : c * nb + s + 1, :] = piece.astype(F32)
        return field[...]

    def by_patch(value, ref):
        field[...] = value
        for c in range(2):
            for s in range(nb):
                ref[c : c + 1, s * block : (s + 1) * block] = field[c * nb + s : c * nb + s + 1, :]

    def wait_bytes(ref, sem):
        pltpu.make_async_copy(ref, ref, sem).wait()

    wait_bytes(index.at[pl.ds(0, narrow_n - 1)], gather_recv.at[0])
    row_group = index.at[pl.ds(my_wide * narrow_n, narrow_n)]
    for j in range(1, wide_n):
        pltpu.make_async_remote_copy(
            src_ref=row_group, dst_ref=row_group,
            send_sem=gather_send.at[1], recv_sem=gather_recv.at[1],
            device_id=wide_peer(j), device_id_type=MESH,
        ).start()

    diag = lax.rem(iota((16, 8 * rank), 0), 8) == lax.div(iota((16, 8 * rank), 1), rank)
    unroll = 8 if tiles % 8 == 0 else 1

    def over_tiles(step):
        def body(i, carry):
            for k in range(unroll):
                step(i * unroll + k)
            return carry

        lax.fori_loop(0, tiles // unroll, body, 0)

    def contract(factor):
        def step(t):
            y = dot_nt(left[rows_at(t * 16, 16), :], factor[rows_at(t * 8 * rank, 8 * rank), :])
            mid[rows_at(t * 16, 16), :] = jnp.where(diag, y, 0.0).astype(BF)

        over_tiles(step)

    def expand(factor, split):
        def step(t):
            y = dot_nn(mid[rows_at(t * 16, 16), :], factor[rows_at(t * 8 * rank, 8 * rank), :])
            high = y.astype(BF)
            terms[rows_at(t * 16, 16), :] = high
            if split:
                terms_low[rows_at(t * 16, 16), :] = (y - high.astype(F32)).astype(BF)

        over_tiles(step)

    wide_y, wide_c = wide_n // 2, 2
    narrow_x = 4 if narrow_n % 4 == 0 and narrow_n > 4 else 2
    narrow_z = narrow_n // narrow_x
    extents = (wide_y, wide_c, narrow_x, narrow_z)
    shifted_wide = {
        (dy, dc): lax.rem(my_wide // wide_c + dy, wide_y) * wide_c + lax.rem(my_wide % wide_c + dc, wide_c)
        for dy in range(wide_y)
        for dc in range(wide_c)
    }
    shifted_narrow = {
        (dx, dz): lax.rem(my_narrow // narrow_z + dx, narrow_x) * narrow_z
        + lax.rem(my_narrow % narrow_z + dz, narrow_z)
        for dx in range(narrow_x)
        for dz in range(narrow_z)
    }

    def send_all(n):
        for dy, dc, dx, dz in far_first(extents):
            to_wide, to_narrow = shifted_wide[dy, dc], shifted_narrow[dx, dz]
            pltpu.make_async_remote_copy(
                src_ref=sent.at[n, to_wide * narrow_n + to_narrow], dst_ref=got.at[n, me],
                send_sem=send_sem.at[n], recv_sem=recv_sem.at[n],
                device_id=(to_wide, to_narrow), device_id_type=MESH,
            ).start()
        got[n, me] = sent[n, me]

    def stage(n, sel, right):
        parts = max(1, rep_rows // 256)
        size = rep_rows // parts

        def body(i, carry):
            y = dot_nn(sel[rows_at(i * size, size), :], right)
            y = y.reshape(size // per, per, block)
            y = jnp.concatenate([y[:, :, :half], y[:, :, half:]], axis=1)
            sent[n, rows_at(i * (size // per), size // per)] = y.astype(BF)
            return carry

        lax.fori_loop(0, parts, body, 0)

    def land(n):
        wait_bytes(got.at[n, pl.ds(0, devices - 1)], recv_sem.at[n])
        y = got[n].astype(F32)
        y = jnp.concatenate([y[:, :per, :], y[:, per:, :]], axis=2)
        flat[...] = y.reshape(rep_rows, block).astype(BF)

    def send_rates(n, x):
        stage(n, reply_sel, jnp.concatenate([x] * cap, axis=0))
        send_all(n)

    def near_part(x):
        near_x = dot_nn(near_cols[...], x).astype(BF)
        parts = max(1, near_rows // 256)
        size = near_rows // parts

        def place_body(i, carry):
            near_left[rows_at(i * size, size), :] = dot_nn(
                near_place[rows_at(i * size, size), :], near_x
            ).astype(BF)
            return carry

        lax.fori_loop(0, parts, place_body, 0)
        steps = 4

        def body(i, acc):
            for k in range(steps):
                g = i * steps + k
                acc = acc + dot_nt(
                    near_left[rows_at(g * 2 * nb, 2 * nb), :], near[rows_at(g * block, block), :]
                )
            return acc

        return lax.fori_loop(0, near_n // steps, body, jnp.zeros((2 * nb, block), F32))

    def row_rates(x):
        left[...] = dot_nn(row_sel[...], x).astype(BF)

    def send_back(n):
        stage(n, col_sel_t, terms[...])
        send_all(n)

    def finish(n_rates, n_back, total):
        land(n_rates)
        left[...] = dot_nn(col_sel[...], flat[...]).astype(BF)
        contract(v)
        expand(u, True)
        total = total + dot_nn(row_sel_t[...], terms[...])
        total = total + dot_nn(row_sel_t[...], terms_low[...])
        land(n_back)
        return total + dot_nn(reply_sel_t[...], flat[...])

    x = by_block(slip).astype(BF)
    row_rates(x)
    loads[0].wait()
    contract(u)

    wait_bytes(index.at[pl.ds(0, (wide_n - 1) * narrow_n)], gather_recv.at[1])
    part = min(32, devices)
    for q in range(0, devices, part):
        wanted = jnp.concatenate(
            [index[q : q + part, r, :] for r in range(index_rows)], axis=1
        )[:, :adm]
        val = jnp.zeros((part, adm), F32)
        for s in range(nb):
            val = jnp.where(wanted == home[s], float(s + 1), val)
        slot_val[q : q + part, :] = val
        pair_hot[q : q + part, :] = hot(val > 0.0)
    order[...] = dot_nn(pair_hot[...], tri[...])
    lane_k = lax.div(iota((devices, 2 * nb * cap), 1), 2 * nb)
    lane_s = lax.rem(iota((devices, 2 * nb * cap), 1), nb) + 1
    chosen = jnp.zeros((devices, 2 * nb * cap), F32)
    for k in range(cap):
        slot_k = jnp.sum(
            jnp.where(order[...] == float(k), slot_val[...], 0.0), axis=1, keepdims=True
        )
        chosen = jnp.where(lane_k == k, slot_k, chosen)
    asked = jnp.where(chosen == lane_s.astype(F32), 1.0, 0.0)
    lanes = 2 * nb * cap
    reply_row = lax.rem(iota((rep_rows, lanes), 0), per)
    reply_mask = reply_row == lax.div(iota((rep_rows, lanes), 1), nb)
    reply_sel[...] = jnp.where(reply_mask, dot_nn(rep[...], asked.astype(BF)), 0.0).astype(BF)
    send_rates(0, x)

    reply_col = lax.rem(iota((lanes, rep_rows), 1), per)
    back_mask = reply_col == lax.div(iota((lanes, rep_rows), 0), nb)
    back_sel = jnp.where(back_mask, dot_nt(asked.T.astype(BF), rep[...]), 0.0)
    summed = back_sel[: 2 * nb]
    for k in range(1, cap):
        summed = summed + back_sel[2 * nb * k : 2 * nb * (k + 1)]
    reply_sel_t[...] = summed.astype(BF)

    for q in range(0, devices, part):
        homes = index[q : q + part, index_rows, :]
        found = jnp.zeros((part, adm), F32)
        for s in range(nb):
            found = jnp.where(homes[:, s : s + 1] == far_cols, 1.0, found)
        slot_val[q : q + part, :] = found
        pair_hot[q : q + part, :] = found.astype(BF)
    order[...] = dot_nn(pair_hot[...], tri[...])
    found = slot_val[...]
    owner = jnp.sum(found * iota((devices, adm), 0).astype(F32), axis=0, keepdims=True)
    place_in = jnp.sum(found * order[...], axis=0, keepdims=True)
    both = jnp.concatenate([owner, place_in, jnp.zeros((6, adm), F32)], axis=0).astype(BF)
    to_row = dot_nt(both, slot_hot[...])
    to_row = (to_row[0:1] * per + to_row[1:2] * 2).astype(I32)
    to_row = to_row + lax.rem(lax.div(iota((1, cols2), 1), 8), 2)
    col_sel_t[...] = hot(iota((rep_rows, cols2), 0) == to_row)
    to_col = dot_nt(slot_hot[...], both)
    to_col = (to_col[:, 0:1] * per + to_col[:, 1:2] * 2).astype(I32)
    to_col = to_col + lax.rem(lax.div(iota((cols2, 1), 0), 8), 2)
    col_sel[...] = hot(iota((cols2, rep_rows), 1) == to_col)

    loads[1].wait()
    expand(v, False)
    send_back(1)
    loads[2].wait()
    first = finish(0, 1, near_part(x))
    by_patch(first, first_out)

    x = (x.astype(F32) * jnp.exp(jnp.tanh(first / by_block(effect)))).astype(BF)
    send_rates(2, x)
    row_rates(x)
    contract(u)
    expand(v, False)
    send_back(3)
    by_patch(finish(2, 3, near_part(x)), second_out)

    wait_bytes(index.at[pl.ds(0, narrow_n - 1)], gather_send.at[0])
    wait_bytes(index.at[pl.ds(0, (wide_n - 1) * narrow_n)], gather_send.at[1])
    for n in range(4):
        wait_bytes(sent.at[n, pl.ds(0, devices - 1)], send_sem.at[n])


def local(slip, effect_stress, home_blocks, far_list, u_factor, v_factor, near_list, near_block):
    wide_n, narrow_n = lax.axis_size("wide"), lax.axis_size("narrow")
    devices = wide_n * narrow_n
    nb = home_blocks.shape[0]
    block = slip.shape[1] // nb
    adm, rank, _ = u_factor.shape
    near_n = near_list.shape[1]
    cap = max(2, adm // devices + 1)
    per = 2 * cap
    rep_rows = devices * per
    cols2 = 2 * adm
    index_rows = -(-adm // 128)
    dims = (wide_n, narrow_n, nb, cap, adm, near_n, block, rank)
    vmem = pl.BlockSpec(memory_space=pltpu.VMEM)
    smem = pl.BlockSpec(memory_space=pltpu.SMEM)
    hbm = pl.BlockSpec(memory_space=pl.ANY)
    field = jax.ShapeDtypeStruct((2, nb * block), F32)
    dma = pltpu.SemaphoreType.DMA
    return pl.pallas_call(
        functools.partial(kernel, dims),
        out_shape=(field, field),
        in_specs=[smem, vmem, vmem, vmem, vmem, hbm, hbm, hbm],
        out_specs=(vmem, vmem),
        scratch_shapes=[
            pltpu.VMEM((adm * rank, block), BF),
            pltpu.VMEM((adm * rank, block), BF),
            pltpu.VMEM((near_n * block, block), BF),
            pltpu.VMEM((devices, index_rows + 1, 128), I32),
            pltpu.VMEM((devices, adm), BF),
            pltpu.VMEM((devices, adm), F32),
            pltpu.VMEM((devices, adm), F32),
            pltpu.VMEM((adm, adm), BF),
            pltpu.VMEM((cols2, adm), BF),
            pltpu.VMEM((cols2, 2 * nb), BF),
            pltpu.VMEM((2 * nb, cols2), BF),
            pltpu.VMEM((near_n * 2 * nb, 2 * near_n), BF),
            pltpu.VMEM((2 * near_n, 2 * nb), BF),
            pltpu.VMEM((near_n * 2 * nb, block), BF),
            pltpu.VMEM((cols2, rep_rows), BF),
            pltpu.VMEM((rep_rows, cols2), BF),
            pltpu.VMEM((rep_rows, 2 * nb * cap), BF),
            pltpu.VMEM((2 * nb, rep_rows), BF),
            pltpu.VMEM((rep_rows, devices), BF),
            pltpu.VMEM((cols2, block), BF),
            pltpu.VMEM((cols2, 8 * rank), BF),
            pltpu.VMEM((cols2, block), BF),
            pltpu.VMEM((cols2, block), BF),
            pltpu.VMEM((rep_rows, block), BF),
            pltpu.VMEM((4, devices, 2 * per, block // 2), BF),
            pltpu.VMEM((4, devices, 2 * per, block // 2), BF),
            pltpu.VMEM((2 * nb, block), F32),
            dma((3,)),
            dma((2,)),
            dma((2,)),
            dma((4,)),
            dma((4,)),
        ],
        compiler_params=pltpu.CompilerParams(
            collective_id=0, has_side_effects=True, vmem_limit_bytes=56 << 20
        ),
        name="stress_two_steps",
    )(
        home_blocks,
        far_list,
        near_list,
        slip,
        effect_stress,
        u_factor.reshape(adm * rank, block),
        v_factor.reshape(adm * rank, block),
        near_block.reshape(near_n * block, block),
    )


def solution(mesh):
    in_specs = (
        P(None, AXES),
        P(None, AXES),
        P(AXES),
        P(None, AXES),
        P(AXES, None, None),
        P(AXES, None, None),
        P(None, AXES),
        P(AXES, None, None),
    )
    out_specs = (P(None, AXES), P(None, AXES))
    return jax.shard_map(local, mesh=mesh, in_specs=in_specs, out_specs=out_specs, check_vma=False)
```

```python
import functools
import itertools

import jax
import jax.numpy as jnp
from jax import lax
from jax.experimental import pallas as pl
from jax.experimental.pallas import tpu as pltpu
from jax.sharding import PartitionSpec as P

AXES = ("wide", "narrow")
MESH = pl.DeviceIdType.MESH
BF = jnp.bfloat16
F32 = jnp.float32
I32 = jnp.int32
WORD_HALF = 1 << 16
NO_BLOCK = 32767


def dot_nt(a, b):
    return lax.dot_general(a, b, (((1,), (1,)), ((), ())), preferred_element_type=F32)


def dot_nn(a, b):
    return lax.dot_general(a, b, (((1,), (0,)), ((), ())), preferred_element_type=F32)


def hot(mask):
    return jnp.where(mask, 1.0, 0.0).astype(BF)


def iota(shape, dim):
    return lax.broadcasted_iota(I32, shape, dim)


def near_first(extents):
    def hops(shift):
        return sum(min(d, n - d) for d, n, core in zip(shift, extents, (0, 1, 0, 0)) if not core)

    shifts = sorted(itertools.product(*map(range, extents)), key=hops)
    back = [shifts.index(tuple(-d % n for d, n in zip(s, extents))) for s in shifts]
    return shifts, back


def over(x, n):
    return x >> (n.bit_length() - 1)


def within(x, n):
    return x & (n - 1)


def rows_at(start, size):
    return pl.ds(pl.multiple_of(start, size), size)


def kernel(
    dims,
    home_hbm, far_hbm, near_list_hbm, slip_hbm, effect_hbm, u_hbm, v_hbm, near_hbm,
    first_hbm, second_hbm,
    home, far, near_list, slip, effect, first_out, second_out,
    u, v, near, index, pair_hot, slot_val, tri, tri_t, far_col, slot_hot, row_sel, row_sel_t,
    near_cols, near_rows, near_left, near_high, near_low, col_sel, col_sel_t, reply_sel, reply_sel_t, rep,
    left, mid, terms, terms_low, flat,
    sent, got, field, scale,
    small_sem, out_sem, load_sem, index_send, index_recv, send_sem, recv_sem,
):
    wide_n, narrow_n, nb, cap, adm, near_n, block, rank = dims
    devices = wide_n * narrow_n
    tiles = adm // 8
    cols2 = 2 * adm
    per = 2 * cap
    index_rows = index.shape[1]
    col_rows = -(-adm // 128)
    half = block // 2
    my_wide = lax.axis_index("wide")
    my_narrow = lax.axis_index("narrow")

    lists = [
        pltpu.make_async_copy(home_hbm, home, small_sem.at[0]),
        pltpu.make_async_copy(far_hbm, far, small_sem.at[1]),
        pltpu.make_async_copy(near_list_hbm, near_list, small_sem.at[2]),
        pltpu.make_async_copy(slip_hbm, slip, small_sem.at[3]),
        pltpu.make_async_copy(effect_hbm, effect, small_sem.at[4]),
    ]
    for load in lists:
        load.start()
    wide_y, wide_c = wide_n // 2, 2
    narrow_x = 4 if narrow_n % 4 == 0 and narrow_n > 4 else 2
    narrow_z = narrow_n // narrow_x
    shifted_wide = {
        (dy, dc): lax.rem(my_wide // wide_c + dy, wide_y) * wide_c + lax.rem(my_wide % wide_c + dc, wide_c)
        for dy in range(wide_y)
        for dc in range(wide_c)
    }
    shifted_narrow = {
        (dx, dz): lax.rem(my_narrow // narrow_z + dx, narrow_x) * narrow_z
        + lax.rem(my_narrow % narrow_z + dz, narrow_z)
        for dx in range(narrow_x)
        for dz in range(narrow_z)
    }
    shifts, back = near_first((wide_y, wide_c, narrow_x, narrow_z))
    device_at = [(shifted_wide[dy, dc], shifted_narrow[dx, dz]) for dy, dc, dx, dz in shifts]
    far_to_near = range(devices - 1, 0, -1)
    group = devices // 2
    part = min(32, group)

    barrier = pltpu.get_barrier_semaphore()
    for p in far_to_near:
        pl.semaphore_signal(barrier, inc=1, device_id=device_at[p], device_id_type=MESH)

    loads = [
        pltpu.make_async_copy(u_hbm, u, load_sem.at[0]),
        pltpu.make_async_copy(v_hbm, v, load_sem.at[1]),
        pltpu.make_async_copy(near_hbm, near, load_sem.at[2]),
    ]
    for load in loads:
        load.start()

    for load in lists:
        load.wait()

    far_cols = far[1:2, :]
    rows = []
    for r in range(col_rows):
        width = min(128, adm - r * 128)
        piece = far_cols[:, r * 128 : r * 128 + width]
        if width < 128:
            piece = jnp.concatenate([piece, jnp.full((1, 128 - width), NO_BLOCK, I32)], axis=1)
        rows.append(piece)
    lane = iota((1, 128), 1)
    home_row = jnp.full((1, 128), NO_BLOCK, I32)
    for s in range(nb):
        home_row = jnp.where(lane == s, home[s], home_row)
    rows += [jnp.full((1, 128), NO_BLOCK, I32)] * (2 * index_rows - col_rows - 1) + [home_row]
    for r in range(index_rows):
        index[0, r : r + 1, :] = rows[r] + rows[index_rows + r] * WORD_HALF

    def index_row(start, size, r):
        word = index[start : start + size, r % index_rows, :]
        return word >> 16 if r >= index_rows else word & (WORD_HALF - 1)

    pl.semaphore_wait(barrier, devices - 1)
    for p in range(1, devices):
        pltpu.make_async_remote_copy(
            src_ref=index.at[0], dst_ref=index.at[back[p]],
            send_sem=index_send, recv_sem=index_recv.at[back[p] // group],
            device_id=device_at[p], device_id_type=MESH,
        ).start()

    row_slot = jnp.zeros((1, adm), I32)
    near_row = jnp.zeros((1, near_n), I32)
    near_col = jnp.zeros((1, near_n), I32)
    far_rows = far[0:1, :]
    for s in range(nb):
        row_slot = jnp.where(far_rows == home[s], s, row_slot)
        near_row = jnp.where(near_list[0:1, :] == home[s], s, near_row)
        near_col = jnp.where(near_list[1:2, :] == home[s], s, near_col)
    place = iota((cols2, adm), 0)
    slot_hot[...] = hot(over(place, 16) * 8 + within(place, 8) == far[2:3, :])
    row_hot = hot(row_slot == within(iota((2 * nb, adm), 0), nb))
    pick = dot_nt(slot_hot[...], row_hot)
    comp = within(over(iota((cols2, 2 * nb), 0), 8), 2)
    row_sel[...] = jnp.where(comp == over(iota((cols2, 2 * nb), 1), nb), pick, 0.0).astype(BF)
    pick_t = dot_nt(row_hot, slot_hot[...])
    comp_t = within(over(iota((2 * nb, cols2), 1), 8), 2)
    row_sel_t[...] = jnp.where(comp_t == over(iota((2 * nb, cols2), 0), nb), pick_t, 0.0).astype(BF)
    tri[...] = hot(iota((adm, adm), 0) < iota((adm, adm), 1))
    tri_t[...] = hot(iota((adm, adm), 0) > iota((adm, adm), 1))
    col_ids = jnp.concatenate([far_cols.astype(F32), jnp.zeros((7, adm), F32)], axis=0).T
    far_col[...] = jnp.broadcast_to(col_ids[:, 0:1].astype(I32), (adm, devices))

    near_place = iota((2 * near_n, near_n), 0)
    near_hot = hot(over(near_place, 16) * 8 + within(near_place, 8) == near_list[2:3, :])
    block_of = within(iota((2 * nb, near_n), 0), nb)
    near_pick = dot_nt(near_hot, hot(near_col == block_of))
    comp = within(over(iota((2 * near_n, 2 * nb), 0), 8), 2)
    near_cols[...] = jnp.where(
        comp == over(iota((2 * near_n, 2 * nb), 1), nb), near_pick, 0.0
    ).astype(BF)
    near_pick_t = dot_nt(hot(near_row == block_of), near_hot)
    comp_t = within(over(iota((2 * nb, 2 * near_n), 1), 8), 2)
    near_rows[...] = jnp.where(
        comp_t == over(iota((2 * nb, 2 * near_n), 0), nb), near_pick_t, 0.0
    ).astype(BF)

    rep_rows = devices * per
    rep[...] = hot(over(iota((group * per, group), 0), per) == iota((group * per, group), 1))

    def by_block(ref):
        for c in range(2):
            for s in range(nb):
                piece = ref[c : c + 1, s * block : (s + 1) * block]
                field[c * nb + s : c * nb + s + 1, :] = piece.astype(F32)
        return field[...]

    def by_patch(value, ref):
        field[...] = value
        for c in range(2):
            for s in range(nb):
                ref[c : c + 1, s * block : (s + 1) * block] = field[c * nb + s : c * nb + s + 1, :]

    def wait_bytes(ref, sem):
        pltpu.make_async_copy(ref, ref, sem).wait()

    diag = within(iota((16, 8 * rank), 0), 8) == over(iota((16, 8 * rank), 1), rank)
    unroll = 16 if tiles % 16 == 0 else 1

    def over_tiles(step):
        def body(i, carry):
            for k in range(unroll):
                step(i * unroll + k)
            return carry

        lax.fori_loop(0, tiles // unroll, body, 0)

    def contract(factor):
        def step(t):
            y = dot_nt(left[rows_at(t * 16, 16), :], factor[rows_at(t * 8 * rank, 8 * rank), :])
            mid[rows_at(t * 16, 16), :] = jnp.where(diag, y, 0.0).astype(BF)

        over_tiles(step)

    def expand(factor, split):
        def step(t):
            y = dot_nn(mid[rows_at(t * 16, 16), :], factor[rows_at(t * 8 * rank, 8 * rank), :])
            high = y.astype(BF)
            terms[rows_at(t * 16, 16), :] = high
            if split:
                terms_low[rows_at(t * 16, 16), :] = (y - high.astype(F32)).astype(BF)

        over_tiles(step)

    def exchange(n, sel, right, order):
        for i in order:
            y = dot_nn(sel[i * part * per : (i + 1) * part * per, :], right)
            y = y.reshape(part, per, block)
            y = jnp.concatenate([y[:, :, :half], y[:, :, half:]], axis=1)
            sent[n, i * part : (i + 1) * part] = y.astype(BF)
            for p in range((i + 1) * part - 1, i * part - 1, -1):
                if p == 0:
                    got[n, 0] = sent[n, 0]
                    continue
                pltpu.make_async_remote_copy(
                    src_ref=sent.at[n, p], dst_ref=got.at[n, back[p]],
                    send_sem=send_sem.at[n], recv_sem=recv_sem.at[n],
                    device_id=device_at[p], device_id_type=MESH,
                ).start()

    parts = devices // part
    far_parts = range(parts - 1, -1, -1)

    def land(n):
        wait_bytes(got.at[n, pl.ds(0, devices - 1)], recv_sem.at[n])
        y = got[n].astype(F32)
        y = jnp.concatenate([y[:, :per, :], y[:, per:, :]], axis=2)
        flat[...] = y.reshape(rep_rows, block).astype(BF)

    def send_rates(n, x, order):
        exchange(n, reply_sel, jnp.concatenate([x] * cap, axis=0), order)

    def near_part(x):
        near_left[...] = dot_nn(near_cols[...], x).astype(BF)
        which = within(iota((16, block), 0), 8)
        steps = 2 if near_n % 16 == 0 else 1

        def body(i, carry):
            for k in range(steps):
                t = i * steps + k
                x_tile = near_left[rows_at(t * 16, 16), :]
                y = jnp.zeros((16, block), F32)
                for j in range(8):
                    term = dot_nt(x_tile, near[pl.ds(pl.multiple_of((t * 8 + j) * block, block), block), :])
                    y = jnp.where(which == j, term, y)
                high = y.astype(BF)
                near_high[rows_at(t * 16, 16), :] = high
                near_low[rows_at(t * 16, 16), :] = (y - high.astype(F32)).astype(BF)
            return carry

        lax.fori_loop(0, near_n // (8 * steps), body, 0)
        return dot_nn(near_rows[...], near_high[...]) + dot_nn(near_rows[...], near_low[...])

    def row_rates(x):
        left[...] = dot_nn(row_sel[...], x).astype(BF)

    def send_back(n):
        exchange(n, col_sel_t, terms[...], far_parts)

    def finish(n_rates, n_back, total):
        land(n_rates)
        left[...] = dot_nn(col_sel[...], flat[...]).astype(BF)
        contract(v)
        expand(u, True)
        total = total + dot_nn(row_sel_t[...], terms[...])
        total = total + dot_nn(row_sel_t[...], terms_low[...])
        land(n_back)
        return total + dot_nn(reply_sel_t[...], flat[...])

    scale[...] = by_block(effect)
    x = by_block(slip).astype(BF)
    row_rates(x)
    loads[0].wait()
    contract(u)

    loads[1].wait()
    expand(v, False)

    lanes = 2 * nb * cap
    lane_k = over(iota((group, lanes), 1), 2 * nb)
    lane_s = within(iota((group, lanes), 1), nb) + 1
    reply_mask = within(iota((group * per, lanes), 0), per) == over(iota((group * per, lanes), 1), nb)
    for h in range(2):
        wait_bytes(index.at[pl.ds(0, group - 1 + h)], index_recv.at[h])
        first_of, end = h * group, (h + 1) * group
        for q in range(first_of, end, part):
            wanted = jnp.concatenate(
                [index_row(q, part, r) for r in range(col_rows)], axis=1
            )[:, :adm]
            val = jnp.zeros((part, adm), F32)
            for s in range(nb):
                val = jnp.where(wanted == home[s], float(s + 1), val)
            slot_val[q : q + part, :] = val
            pair_hot[q : q + part, :] = hot(val > 0.0)
        ranks = dot_nn(pair_hot[first_of:end, :], tri[...])
        chosen = jnp.zeros((group, lanes), F32)
        for k in range(cap):
            slot_k = jnp.sum(
                jnp.where(ranks == float(k), slot_val[first_of:end, :], 0.0), axis=1, keepdims=True
            )
            chosen = jnp.where(lane_k == k, slot_k, chosen)
        wants = jnp.where(chosen == lane_s.astype(F32), 1.0, 0.0)
        spread = dot_nn(rep[...], wants.astype(BF))
        reply_sel[first_of * per : end * per, :] = jnp.where(reply_mask, spread, 0.0).astype(BF)
        send_rates(0, x, range(h * parts // 2, (h + 1) * parts // 2))

    homes = index_row(0, devices, 2 * index_rows - 1).astype(F32).T.astype(I32)
    tall = 128 if adm % 128 == 0 else adm
    founds = []
    for q in range(0, adm, tall):
        ids = far_col[q : q + tall, :]
        found = jnp.zeros((tall, devices), F32)
        for s in range(nb):
            found = jnp.where(ids == homes[s : s + 1, :], 1.0, found)
        founds.append(found.astype(BF))
    found = jnp.concatenate(founds, axis=0)
    place_in = (dot_nn(tri_t[...], found) * found.astype(F32)).astype(BF)
    owner = dot_nt(iota((8, devices), 1).astype(BF), found)
    place_in = dot_nt(jnp.ones((8, devices), BF), place_in)
    both = jnp.concatenate([owner[0:1], place_in[0:1], jnp.zeros((6, adm), F32)], axis=0).astype(BF)
    to_row = dot_nt(both, slot_hot[...])
    to_row = (to_row[0:1] * per + to_row[1:2] * 2).astype(I32)
    to_row = to_row + within(over(iota((1, cols2), 1), 8), 2)
    band = min(128, rep_rows)

    def rows_body(i, carry):
        col_sel_t[rows_at(i * band, band), :] = hot(iota((band, cols2), 0) == to_row - i * band)
        return carry

    lax.fori_loop(0, rep_rows // band, rows_body, 0)
    send_back(1)

    side = 256 if cols2 % 256 == 0 else cols2

    for i in range(0, rep_rows, band):
        for k in range(0, cols2, side):
            col_sel[k : k + side, i : i + band] = col_sel_t[i : i + band, k : k + side].T

    fold = hot(within(iota((2 * nb, lanes), 1), 2 * nb) == iota((2 * nb, lanes), 0))
    reply_sel_t[...] = dot_nt(fold, reply_sel[...]).astype(BF)

    loads[2].wait()
    first = finish(0, 1, near_part(x))
    x = (x.astype(F32) * jnp.exp(jnp.tanh(first / scale[...]))).astype(BF)
    send_rates(2, x, far_parts)
    by_patch(first, first_out)
    first_copy = pltpu.make_async_copy(first_out, first_hbm, out_sem.at[0])
    first_copy.start()
    row_rates(x)
    contract(u)
    expand(v, False)
    send_back(3)
    by_patch(finish(2, 3, near_part(x)), second_out)
    second_copy = pltpu.make_async_copy(second_out, second_hbm, out_sem.at[1])
    second_copy.start()

    wait_bytes(index.at[pl.ds(0, devices - 1)], index_send)
    first_copy.wait()
    second_copy.wait()
    for n in range(4):
        wait_bytes(sent.at[n, pl.ds(0, devices - 1)], send_sem.at[n])


def hand_out(first_in, second_in, first_out, second_out):
    first_out[...] = first_in[...]
    second_out[...] = second_in[...]


def local(slip, effect_stress, home_blocks, far_list, u_factor, v_factor, near_list, near_block):
    wide_n, narrow_n = lax.axis_size("wide"), lax.axis_size("narrow")
    devices = wide_n * narrow_n
    nb = home_blocks.shape[0]
    block = slip.shape[1] // nb
    adm, rank, _ = u_factor.shape
    near_n = near_list.shape[1]
    cap = max(2, adm // devices + 1)
    per = 2 * cap
    rep_rows = devices * per
    cols2 = 2 * adm
    index_rows = (-(-adm // 128) + 2) // 2
    dims = (wide_n, narrow_n, nb, cap, adm, near_n, block, rank)
    vmem = pl.BlockSpec(memory_space=pltpu.VMEM)
    hbm = pl.BlockSpec(memory_space=pl.ANY)
    field = jax.ShapeDtypeStruct((2, nb * block), F32)
    dma = pltpu.SemaphoreType.DMA
    results = pl.pallas_call(
        functools.partial(kernel, dims),
        out_shape=(field, field),
        in_specs=[hbm] * 8,
        out_specs=(hbm, hbm),
        scratch_shapes=[
            pltpu.SMEM(home_blocks.shape, I32),
            pltpu.VMEM(far_list.shape, I32),
            pltpu.VMEM(near_list.shape, I32),
            pltpu.VMEM(slip.shape, BF),
            pltpu.VMEM(slip.shape, F32),
            pltpu.VMEM(slip.shape, F32),
            pltpu.VMEM(slip.shape, F32),
            pltpu.VMEM((adm * rank, block), BF),
            pltpu.VMEM((adm * rank, block), BF),
            pltpu.VMEM((near_n * block, block), BF),
            pltpu.VMEM((devices, index_rows, 128), I32),
            pltpu.VMEM((devices, adm), BF),
            pltpu.VMEM((devices, adm), F32),
            pltpu.VMEM((adm, adm), BF),
            pltpu.VMEM((adm, adm), BF),
            pltpu.VMEM((adm, devices), I32),
            pltpu.VMEM((cols2, adm), BF),
            pltpu.VMEM((cols2, 2 * nb), BF),
            pltpu.VMEM((2 * nb, cols2), BF),
            pltpu.VMEM((2 * near_n, 2 * nb), BF),
            pltpu.VMEM((2 * nb, 2 * near_n), BF),
            pltpu.VMEM((2 * near_n, block), BF),
            pltpu.VMEM((2 * near_n, block), BF),
            pltpu.VMEM((2 * near_n, block), BF),
            pltpu.VMEM((cols2, rep_rows), BF),
            pltpu.VMEM((rep_rows, cols2), BF),
            pltpu.VMEM((rep_rows, 2 * nb * cap), BF),
            pltpu.VMEM((2 * nb, rep_rows), BF),
            pltpu.VMEM((rep_rows // 2, devices // 2), BF),
            pltpu.VMEM((cols2, block), BF),
            pltpu.VMEM((cols2, 8 * rank), BF),
            pltpu.VMEM((cols2, block), BF),
            pltpu.VMEM((cols2, block), BF),
            pltpu.VMEM((rep_rows, block), BF),
            pltpu.VMEM((4, devices, 2 * per, block // 2), BF),
            pltpu.VMEM((4, devices, 2 * per, block // 2), BF),
            pltpu.VMEM((2 * nb, block), F32),
            pltpu.VMEM((2 * nb, block), F32),
            dma((5,)),
            dma((2,)),
            dma((3,)),
            dma(()),
            dma((2,)),
            dma((4,)),
            dma((4,)),
        ],
        compiler_params=pltpu.CompilerParams(
            collective_id=0, has_side_effects=True, vmem_limit_bytes=56 << 20
        ),
        name="stress_two_steps",
    )(
        home_blocks,
        far_list,
        near_list,
        slip,
        effect_stress,
        u_factor.reshape(adm * rank, block),
        v_factor.reshape(adm * rank, block),
        near_block.reshape(near_n * block, block),
    )
    return pl.pallas_call(
        hand_out,
        out_shape=(field, field),
        in_specs=[vmem, vmem],
        out_specs=(vmem, vmem),
        name="hand_out",
    )(*results)


def solution(mesh):
    in_specs = (
        P(None, AXES),
        P(None, AXES),
        P(AXES),
        P(None, AXES),
        P(AXES, None, None),
        P(AXES, None, None),
        P(None, AXES),
        P(AXES, None, None),
    )
    out_specs = (P(None, AXES), P(None, AXES))
    return jax.shard_map(local, mesh=mesh, in_specs=in_specs, out_specs=out_specs, check_vma=False)
```

```python
import functools
import itertools

import jax
import jax.numpy as jnp
from jax import lax
from jax.experimental import pallas as pl
from jax.experimental.pallas import tpu as pltpu
from jax.sharding import PartitionSpec as P

AXES = ("wide", "narrow")
MESH = pl.DeviceIdType.MESH
BF = jnp.bfloat16
F32 = jnp.float32
I32 = jnp.int32
WORD_HALF = 1 << 16
NO_BLOCK = 32767


def dot_nt(a, b):
    return lax.dot_general(a, b, (((1,), (1,)), ((), ())), preferred_element_type=F32)


def dot_nn(a, b):
    return lax.dot_general(a, b, (((1,), (0,)), ((), ())), preferred_element_type=F32)


def hot(mask):
    return jnp.where(mask, 1.0, 0.0).astype(BF)


def iota(shape, dim):
    return lax.broadcasted_iota(I32, shape, dim)


def near_first(extents):
    def hops(shift):
        return sum(min(d, n - d) for d, n, core in zip(shift, extents, (0, 1, 0, 0)) if not core)

    shifts = sorted(itertools.product(*map(range, extents)), key=hops)
    back = [shifts.index(tuple(-d % n for d, n in zip(s, extents))) for s in shifts]
    return shifts, back


def over(x, n):
    return x >> (n.bit_length() - 1)


def within(x, n):
    return x & (n - 1)


def rows_at(start, size):
    return pl.ds(pl.multiple_of(start, size), size)


def kernel(
    dims,
    home_hbm, far_hbm, near_list_hbm, slip_hbm, effect_hbm, u_hbm, v_hbm, near_hbm,
    first_hbm, second_hbm,
    home, far, near_list, slip, effect, first_out, second_out,
    u, v, near, index, pair_hot, slot_val, tri, tri_t, far_col, slot_hot, row_sel, row_sel_t,
    near_cols, near_rows, near_left, near_high, near_low, col_sel, col_sel_t, reply_sel, reply_sel_t, rep,
    left, mid, terms, terms_low, flat,
    sent, got, field, scale,
    small_sem, out_sem, load_sem, index_send, index_recv, send_sem, recv_sem,
):
    wide_n, narrow_n, nb, cap, adm, near_n, block, rank = dims
    devices = wide_n * narrow_n
    tiles = adm // 8
    cols2 = 2 * adm
    per = 2 * cap
    index_rows = index.shape[1]
    col_rows = -(-adm // 128)
    half = block // 2
    my_wide = lax.axis_index("wide")
    my_narrow = lax.axis_index("narrow")

    lists = [
        pltpu.make_async_copy(home_hbm, home, small_sem.at[0]),
        pltpu.make_async_copy(far_hbm, far, small_sem.at[1]),
        pltpu.make_async_copy(near_list_hbm, near_list, small_sem.at[2]),
        pltpu.make_async_copy(slip_hbm, slip, small_sem.at[3]),
        pltpu.make_async_copy(effect_hbm, effect, small_sem.at[4]),
    ]
    for load in lists:
        load.start()
    wide_y, wide_c = wide_n // 2, 2
    narrow_x = 4 if narrow_n % 4 == 0 and narrow_n > 4 else 2
    narrow_z = narrow_n // narrow_x
    shifted_wide = {
        (dy, dc): lax.rem(my_wide // wide_c + dy, wide_y) * wide_c + lax.rem(my_wide % wide_c + dc, wide_c)
        for dy in range(wide_y)
        for dc in range(wide_c)
    }
    shifted_narrow = {
        (dx, dz): lax.rem(my_narrow // narrow_z + dx, narrow_x) * narrow_z
        + lax.rem(my_narrow % narrow_z + dz, narrow_z)
        for dx in range(narrow_x)
        for dz in range(narrow_z)
    }
    shifts, back = near_first((wide_y, wide_c, narrow_x, narrow_z))
    device_at = [(shifted_wide[dy, dc], shifted_narrow[dx, dz]) for dy, dc, dx, dz in shifts]
    far_to_near = range(devices - 1, 0, -1)
    group = devices // 2
    part = min(32, group)

    barrier = pltpu.get_barrier_semaphore()
    for p in far_to_near:
        pl.semaphore_signal(barrier, inc=1, device_id=device_at[p], device_id_type=MESH)

    loads = [
        pltpu.make_async_copy(u_hbm, u, load_sem.at[0]),
        pltpu.make_async_copy(v_hbm, v, load_sem.at[1]),
        pltpu.make_async_copy(near_hbm, near, load_sem.at[2]),
    ]
    for load in loads:
        load.start()

    for load in lists:
        load.wait()

    far_cols = far[1:2, :]
    rows = []
    for r in range(col_rows):
        width = min(128, adm - r * 128)
        piece = far_cols[:, r * 128 : r * 128 + width]
        if width < 128:
            piece = jnp.concatenate([piece, jnp.full((1, 128 - width), NO_BLOCK, I32)], axis=1)
        rows.append(piece)
    lane = iota((1, 128), 1)
    home_row = jnp.full((1, 128), NO_BLOCK, I32)
    for s in range(nb):
        home_row = jnp.where(lane == s, home[s], home_row)
    rows += [jnp.full((1, 128), NO_BLOCK, I32)] * (2 * index_rows - col_rows - 1) + [home_row]
    for r in range(index_rows):
        index[0, r : r + 1, :] = rows[r] + rows[index_rows + r] * WORD_HALF

    def index_row(start, size, r):
        word = index[start : start + size, r % index_rows, :]
        return word >> 16 if r >= index_rows else word & (WORD_HALF - 1)

    pl.semaphore_wait(barrier, devices - 1)
    for p in range(1, devices):
        pltpu.make_async_remote_copy(
            src_ref=index.at[0], dst_ref=index.at[back[p]],
            send_sem=index_send, recv_sem=index_recv.at[back[p] // group],
            device_id=device_at[p], device_id_type=MESH,
        ).start()

    row_slot = jnp.zeros((1, adm), I32)
    near_row = jnp.zeros((1, near_n), I32)
    near_col = jnp.zeros((1, near_n), I32)
    far_rows = far[0:1, :]
    for s in range(nb):
        row_slot = jnp.where(far_rows == home[s], s, row_slot)
        near_row = jnp.where(near_list[0:1, :] == home[s], s, near_row)
        near_col = jnp.where(near_list[1:2, :] == home[s], s, near_col)
    place = iota((cols2, adm), 0)
    slot_hot[...] = hot(over(place, 16) * 8 + within(place, 8) == far[2:3, :])
    row_hot = hot(row_slot == within(iota((2 * nb, adm), 0), nb))
    pick = dot_nt(slot_hot[...], row_hot)
    comp = within(over(iota((cols2, 2 * nb), 0), 8), 2)
    row_sel[...] = jnp.where(comp == over(iota((cols2, 2 * nb), 1), nb), pick, 0.0).astype(BF)
    pick_t = dot_nt(row_hot, slot_hot[...])
    comp_t = within(over(iota((2 * nb, cols2), 1), 8), 2)
    row_sel_t[...] = jnp.where(comp_t == over(iota((2 * nb, cols2), 0), nb), pick_t, 0.0).astype(BF)
    tri[...] = hot(iota((adm, adm), 0) < iota((adm, adm), 1))
    tri_t[...] = hot(iota((adm, adm), 0) > iota((adm, adm), 1))
    col_ids = jnp.concatenate([far_cols.astype(F32), jnp.zeros((7, adm), F32)], axis=0).T
    far_col[...] = jnp.broadcast_to(col_ids[:, 0:1].astype(I32), (adm, devices))

    near_place = iota((2 * near_n, near_n), 0)
    near_hot = hot(over(near_place, 16) * 8 + within(near_place, 8) == near_list[2:3, :])
    block_of = within(iota((2 * nb, near_n), 0), nb)
    near_pick = dot_nt(near_hot, hot(near_col == block_of))
    comp = within(over(iota((2 * near_n, 2 * nb), 0), 8), 2)
    near_cols[...] = jnp.where(
        comp == over(iota((2 * near_n, 2 * nb), 1), nb), near_pick, 0.0
    ).astype(BF)
    near_pick_t = dot_nt(hot(near_row == block_of), near_hot)
    comp_t = within(over(iota((2 * nb, 2 * near_n), 1), 8), 2)
    near_rows[...] = jnp.where(
        comp_t == over(iota((2 * nb, 2 * near_n), 0), nb), near_pick_t, 0.0
    ).astype(BF)

    rep_rows = devices * per
    rep[...] = hot(over(iota((group * per, group), 0), per) == iota((group * per, group), 1))

    def by_block(ref):
        for c in range(2):
            for s in range(nb):
                piece = ref[c : c + 1, s * block : (s + 1) * block]
                field[c * nb + s : c * nb + s + 1, :] = piece.astype(F32)
        return field[...]

    def by_patch(value, ref):
        field[...] = value
        for c in range(2):
            for s in range(nb):
                ref[c : c + 1, s * block : (s + 1) * block] = field[c * nb + s : c * nb + s + 1, :]

    def wait_bytes(ref, sem):
        pltpu.make_async_copy(ref, ref, sem).wait()

    diag = within(iota((16, 8 * rank), 0), 8) == over(iota((16, 8 * rank), 1), rank)
    unroll = 24 if tiles % 24 == 0 else 1

    def over_tiles(step):
        def body(i, carry):
            for k in range(unroll):
                step(i * unroll + k)
            return carry

        lax.fori_loop(0, tiles // unroll, body, 0)

    def contract(factor):
        def step(t):
            y = dot_nt(left[rows_at(t * 16, 16), :], factor[rows_at(t * 8 * rank, 8 * rank), :])
            mid[rows_at(t * 16, 16), :] = jnp.where(diag, y, 0.0).astype(BF)

        over_tiles(step)

    def expand(factor, split):
        def step(t):
            y = dot_nn(mid[rows_at(t * 16, 16), :], factor[rows_at(t * 8 * rank, 8 * rank), :])
            high = y.astype(BF)
            terms[rows_at(t * 16, 16), :] = high
            if split:
                terms_low[rows_at(t * 16, 16), :] = (y - high.astype(F32)).astype(BF)

        over_tiles(step)

    def send(n, p):
        pltpu.make_async_remote_copy(
            src_ref=sent.at[n, p], dst_ref=got.at[n, back[p]],
            send_sem=send_sem.at[n], recv_sem=recv_sem.at[n],
            device_id=device_at[p], device_id_type=MESH,
        ).start()

    def exchange(n, sel, right, order, later=False):
        left_over = []
        for i in order:
            y = dot_nn(sel[i * part * per : (i + 1) * part * per, :], right)
            y = y.reshape(part, per, block)
            y = jnp.concatenate([y[:, :, :half], y[:, :, half:]], axis=1)
            sent[n, i * part : (i + 1) * part] = y.astype(BF)
            for p in range((i + 1) * part - 1, i * part - 1, -1):
                if p == 0:
                    got[n, 0] = sent[n, 0]
                elif later:
                    left_over.append((n, p))
                else:
                    send(n, p)
        return left_over

    def send_share(waiting, done, steps):
        for n, p in waiting[len(waiting) * done // steps : len(waiting) * (done + 1) // steps]:
            send(n, p)

    parts = devices // part
    far_parts = range(parts - 1, -1, -1)

    def land(n):
        wait_bytes(got.at[n, pl.ds(0, devices - 1)], recv_sem.at[n])
        y = got[n].astype(F32)
        y = jnp.concatenate([y[:, :per, :], y[:, per:, :]], axis=2)
        flat[...] = y.reshape(rep_rows, block).astype(BF)

    def send_rates(n, x, order, later=False):
        return exchange(n, reply_sel, jnp.concatenate([x] * cap, axis=0), order, later)

    def near_part(x, waiting):
        near_left[...] = dot_nn(near_cols[...], x).astype(BF)
        which = within(iota((16, block), 0), 8)
        for t in range(near_n // 8):
            x_tile = near_left[t * 16 : (t + 1) * 16, :]
            y = jnp.zeros((16, block), F32)
            for j in range(8):
                g = t * 8 + j
                y = jnp.where(which == j, dot_nt(x_tile, near[g * block : (g + 1) * block, :]), y)
                send_share(waiting, g, near_n)
            high = y.astype(BF)
            near_high[t * 16 : (t + 1) * 16, :] = high
            near_low[t * 16 : (t + 1) * 16, :] = (y - high.astype(F32)).astype(BF)
        return dot_nn(near_rows[...], near_high[...]) + dot_nn(near_rows[...], near_low[...])

    def row_rates(x):
        left[...] = dot_nn(row_sel[...], x).astype(BF)

    def send_back(n):
        return exchange(n, col_sel_t, terms[...], far_parts, True)

    def finish(n_rates, n_back, total):
        land(n_rates)
        left[...] = dot_nn(col_sel[...], flat[...]).astype(BF)
        contract(v)
        expand(u, True)
        total = total + dot_nn(row_sel_t[...], terms[...])
        total = total + dot_nn(row_sel_t[...], terms_low[...])
        land(n_back)
        return total + dot_nn(reply_sel_t[...], flat[...])

    scale[...] = by_block(effect)
    x = by_block(slip).astype(BF)
    row_rates(x)
    loads[0].wait()
    contract(u)

    loads[1].wait()
    expand(v, False)

    lanes = 2 * nb * cap
    lane_k = over(iota((group, lanes), 1), 2 * nb)
    lane_s = within(iota((group, lanes), 1), nb) + 1
    reply_mask = within(iota((group * per, lanes), 0), per) == over(iota((group * per, lanes), 1), nb)
    for h in range(2):
        wait_bytes(index.at[pl.ds(0, group - 1 + h)], index_recv.at[h])
        first_of, end = h * group, (h + 1) * group
        for q in range(first_of, end, part):
            wanted = jnp.concatenate(
                [index_row(q, part, r) for r in range(col_rows)], axis=1
            )[:, :adm]
            val = jnp.zeros((part, adm), F32)
            for s in range(nb):
                val = jnp.where(wanted == home[s], float(s + 1), val)
            slot_val[q : q + part, :] = val
            pair_hot[q : q + part, :] = hot(val > 0.0)
        ranks = dot_nn(pair_hot[first_of:end, :], tri[...])
        chosen = jnp.zeros((group, lanes), F32)
        for k in range(cap):
            slot_k = jnp.sum(
                jnp.where(ranks == float(k), slot_val[first_of:end, :], 0.0), axis=1, keepdims=True
            )
            chosen = jnp.where(lane_k == k, slot_k, chosen)
        wants = jnp.where(chosen == lane_s.astype(F32), 1.0, 0.0)
        spread = dot_nn(rep[...], wants.astype(BF))
        reply_sel[first_of * per : end * per, :] = jnp.where(reply_mask, spread, 0.0).astype(BF)
        send_rates(0, x, range(h * parts // 2, (h + 1) * parts // 2))

    homes = index_row(0, devices, 2 * index_rows - 1).astype(F32).T.astype(I32)
    tall = 128 if adm % 128 == 0 else adm
    founds = []
    for q in range(0, adm, tall):
        ids = far_col[q : q + tall, :]
        found = jnp.zeros((tall, devices), F32)
        for s in range(nb):
            found = jnp.where(ids == homes[s : s + 1, :], 1.0, found)
        founds.append(found.astype(BF))
    found = jnp.concatenate(founds, axis=0)
    place_in = (dot_nn(tri_t[...], found) * found.astype(F32)).astype(BF)
    owner = dot_nt(iota((8, devices), 1).astype(BF), found)
    place_in = dot_nt(jnp.ones((8, devices), BF), place_in)
    both = jnp.concatenate([owner[0:1], place_in[0:1], jnp.zeros((6, adm), F32)], axis=0).astype(BF)
    to_row = dot_nt(both, slot_hot[...])
    to_row = (to_row[0:1] * per + to_row[1:2] * 2).astype(I32)
    to_row = to_row + within(over(iota((1, cols2), 1), 8), 2)
    band = min(128, rep_rows)

    def rows_body(i, carry):
        col_sel_t[rows_at(i * band, band), :] = hot(iota((band, cols2), 0) == to_row - i * band)
        return carry

    lax.fori_loop(0, rep_rows // band, rows_body, 0)
    waiting = send_back(1)
    loads[2].wait()
    near_sum = near_part(x, waiting)

    side = 256 if cols2 % 256 == 0 else cols2

    for i in range(0, rep_rows, band):
        for k in range(0, cols2, side):
            col_sel[k : k + side, i : i + band] = col_sel_t[i : i + band, k : k + side].T

    fold = hot(within(iota((2 * nb, lanes), 1), 2 * nb) == iota((2 * nb, lanes), 0))
    reply_sel_t[...] = dot_nt(fold, reply_sel[...]).astype(BF)

    first = finish(0, 1, near_sum)
    x = (x.astype(F32) * jnp.exp(jnp.tanh(first / scale[...]))).astype(BF)
    send_rates(2, x, far_parts)
    by_patch(first, first_out)
    first_copy = pltpu.make_async_copy(first_out, first_hbm, out_sem.at[0])
    first_copy.start()
    row_rates(x)
    contract(u)
    expand(v, False)
    waiting = send_back(3)
    by_patch(finish(2, 3, near_part(x, waiting)), second_out)
    second_copy = pltpu.make_async_copy(second_out, second_hbm, out_sem.at[1])
    second_copy.start()

    wait_bytes(index.at[pl.ds(0, devices - 1)], index_send)
    first_copy.wait()
    second_copy.wait()
    for n in range(4):
        wait_bytes(sent.at[n, pl.ds(0, devices - 1)], send_sem.at[n])


def hand_out(first_in, second_in, first_out, second_out):
    first_out[...] = first_in[...]
    second_out[...] = second_in[...]


def local(slip, effect_stress, home_blocks, far_list, u_factor, v_factor, near_list, near_block):
    wide_n, narrow_n = lax.axis_size("wide"), lax.axis_size("narrow")
    devices = wide_n * narrow_n
    nb = home_blocks.shape[0]
    block = slip.shape[1] // nb
    adm, rank, _ = u_factor.shape
    near_n = near_list.shape[1]
    cap = max(2, adm // devices + 1)
    per = 2 * cap
    rep_rows = devices * per
    cols2 = 2 * adm
    index_rows = (-(-adm // 128) + 2) // 2
    dims = (wide_n, narrow_n, nb, cap, adm, near_n, block, rank)
    vmem = pl.BlockSpec(memory_space=pltpu.VMEM)
    hbm = pl.BlockSpec(memory_space=pl.ANY)
    field = jax.ShapeDtypeStruct((2, nb * block), F32)
    dma = pltpu.SemaphoreType.DMA
    results = pl.pallas_call(
        functools.partial(kernel, dims),
        out_shape=(field, field),
        in_specs=[hbm] * 8,
        out_specs=(hbm, hbm),
        scratch_shapes=[
            pltpu.SMEM(home_blocks.shape, I32),
            pltpu.VMEM(far_list.shape, I32),
            pltpu.VMEM(near_list.shape, I32),
            pltpu.VMEM(slip.shape, BF),
            pltpu.VMEM(slip.shape, F32),
            pltpu.VMEM(slip.shape, F32),
            pltpu.VMEM(slip.shape, F32),
            pltpu.VMEM((adm * rank, block), BF),
            pltpu.VMEM((adm * rank, block), BF),
            pltpu.VMEM((near_n * block, block), BF),
            pltpu.VMEM((devices, index_rows, 128), I32),
            pltpu.VMEM((devices, adm), BF),
            pltpu.VMEM((devices, adm), F32),
            pltpu.VMEM((adm, adm), BF),
            pltpu.VMEM((adm, adm), BF),
            pltpu.VMEM((adm, devices), I32),
            pltpu.VMEM((cols2, adm), BF),
            pltpu.VMEM((cols2, 2 * nb), BF),
            pltpu.VMEM((2 * nb, cols2), BF),
            pltpu.VMEM((2 * near_n, 2 * nb), BF),
            pltpu.VMEM((2 * nb, 2 * near_n), BF),
            pltpu.VMEM((2 * near_n, block), BF),
            pltpu.VMEM((2 * near_n, block), BF),
            pltpu.VMEM((2 * near_n, block), BF),
            pltpu.VMEM((cols2, rep_rows), BF),
            pltpu.VMEM((rep_rows, cols2), BF),
            pltpu.VMEM((rep_rows, 2 * nb * cap), BF),
            pltpu.VMEM((2 * nb, rep_rows), BF),
            pltpu.VMEM((rep_rows // 2, devices // 2), BF),
            pltpu.VMEM((cols2, block), BF),
            pltpu.VMEM((cols2, 8 * rank), BF),
            pltpu.VMEM((cols2, block), BF),
            pltpu.VMEM((cols2, block), BF),
            pltpu.VMEM((rep_rows, block), BF),
            pltpu.VMEM((4, devices, 2 * per, block // 2), BF),
            pltpu.VMEM((4, devices, 2 * per, block // 2), BF),
            pltpu.VMEM((2 * nb, block), F32),
            pltpu.VMEM((2 * nb, block), F32),
            dma((5,)),
            dma((2,)),
            dma((3,)),
            dma(()),
            dma((2,)),
            dma((4,)),
            dma((4,)),
        ],
        compiler_params=pltpu.CompilerParams(
            collective_id=0, has_side_effects=True, vmem_limit_bytes=56 << 20
        ),
        name="stress_two_steps",
    )(
        home_blocks,
        far_list,
        near_list,
        slip,
        effect_stress,
        u_factor.reshape(adm * rank, block),
        v_factor.reshape(adm * rank, block),
        near_block.reshape(near_n * block, block),
    )
    return pl.pallas_call(
        hand_out,
        out_shape=(field, field),
        in_specs=[vmem, vmem],
        out_specs=(vmem, vmem),
        name="hand_out",
    )(*results)


def solution(mesh):
    in_specs = (
        P(None, AXES),
        P(None, AXES),
        P(AXES),
        P(None, AXES),
        P(AXES, None, None),
        P(AXES, None, None),
        P(None, AXES),
        P(AXES, None, None),
    )
    out_specs = (P(None, AXES), P(None, AXES))
    return jax.shard_map(local, mesh=mesh, in_specs=in_specs, out_specs=out_specs, check_vma=False)
```

```python
import functools
import itertools

import jax
import jax.numpy as jnp
from jax import lax
from jax.experimental import pallas as pl
from jax.experimental.pallas import tpu as pltpu
from jax.sharding import PartitionSpec as P

AXES = ("wide", "narrow")
MESH = pl.DeviceIdType.MESH
BF = jnp.bfloat16
F32 = jnp.float32
I32 = jnp.int32
WORD_HALF = 1 << 16
NO_BLOCK = 32767


def dot_nt(a, b):
    return lax.dot_general(a, b, (((1,), (1,)), ((), ())), preferred_element_type=F32)


def dot_nn(a, b):
    return lax.dot_general(a, b, (((1,), (0,)), ((), ())), preferred_element_type=F32)


def hot(mask):
    return jnp.where(mask, 1.0, 0.0).astype(BF)


def iota(shape, dim):
    return lax.broadcasted_iota(I32, shape, dim)


def near_first(extents):
    def hops(shift):
        return sum(min(d, n - d) for d, n, core in zip(shift, extents, (0, 1, 0, 0)) if not core)

    shifts = sorted(itertools.product(*map(range, extents)), key=hops)
    back = [shifts.index(tuple(-d % n for d, n in zip(s, extents))) for s in shifts]
    return shifts, back


def over(x, n):
    return x >> (n.bit_length() - 1)


def within(x, n):
    return x & (n - 1)


def rows_at(start, size):
    return pl.ds(pl.multiple_of(start, size), size)


def kernel(
    dims,
    home_hbm, far_hbm, near_list_hbm, slip_hbm, effect_hbm, u_hbm, v_hbm, near_hbm,
    first_hbm, second_hbm,
    home, far, near_list, slip, effect, first_out, second_out,
    u, v, near, index, pair_hot, slot_val, tri, tri_t, far_col, slot_hot, row_sel, row_sel_t,
    near_cols, near_rows, near_left, near_high, near_low, col_sel, col_sel_t, reply_sel, reply_sel_t, rep,
    left, mid, terms, terms_low, flat,
    sent, got, field, scale,
    small_sem, out_sem, load_sem, index_send, index_recv, send_sem, recv_sem,
):
    wide_n, narrow_n, nb, cap, adm, near_n, block, rank = dims
    devices = wide_n * narrow_n
    tiles = adm // 8
    cols2 = 2 * adm
    per = 2 * cap
    index_rows = index.shape[1]
    col_rows = -(-adm // 128)
    half = block // 2
    my_wide = lax.axis_index("wide")
    my_narrow = lax.axis_index("narrow")

    lists = [
        pltpu.make_async_copy(home_hbm, home, small_sem.at[0]),
        pltpu.make_async_copy(far_hbm, far, small_sem.at[1]),
        pltpu.make_async_copy(near_list_hbm, near_list, small_sem.at[2]),
        pltpu.make_async_copy(slip_hbm, slip, small_sem.at[3]),
        pltpu.make_async_copy(effect_hbm, effect, small_sem.at[4]),
    ]
    for load in lists:
        load.start()
    wide_y, wide_c = wide_n // 2, 2
    narrow_x = 4 if narrow_n % 4 == 0 and narrow_n > 4 else 2
    narrow_z = narrow_n // narrow_x
    shifted_wide = {
        (dy, dc): lax.rem(my_wide // wide_c + dy, wide_y) * wide_c + lax.rem(my_wide % wide_c + dc, wide_c)
        for dy in range(wide_y)
        for dc in range(wide_c)
    }
    shifted_narrow = {
        (dx, dz): lax.rem(my_narrow // narrow_z + dx, narrow_x) * narrow_z
        + lax.rem(my_narrow % narrow_z + dz, narrow_z)
        for dx in range(narrow_x)
        for dz in range(narrow_z)
    }
    shifts, back = near_first((wide_y, wide_c, narrow_x, narrow_z))
    device_at = [(shifted_wide[dy, dc], shifted_narrow[dx, dz]) for dy, dc, dx, dz in shifts]
    far_to_near = range(devices - 1, 0, -1)
    group = devices // 2
    part = min(64, group)

    barrier = pltpu.get_barrier_semaphore()
    for p in far_to_near:
        pl.semaphore_signal(barrier, inc=1, device_id=device_at[p], device_id_type=MESH)

    loads = [
        pltpu.make_async_copy(u_hbm, u, load_sem.at[0]),
        pltpu.make_async_copy(v_hbm, v, load_sem.at[1]),
        pltpu.make_async_copy(near_hbm, near, load_sem.at[2]),
    ]
    for load in loads:
        load.start()

    for load in lists:
        load.wait()

    far_cols = far[1:2, :]
    rows = []
    for r in range(col_rows):
        width = min(128, adm - r * 128)
        piece = far_cols[:, r * 128 : r * 128 + width]
        if width < 128:
            piece = jnp.concatenate([piece, jnp.full((1, 128 - width), NO_BLOCK, I32)], axis=1)
        rows.append(piece)
    lane = iota((1, 128), 1)
    home_row = jnp.full((1, 128), NO_BLOCK, I32)
    for s in range(nb):
        home_row = jnp.where(lane == s, home[s], home_row)
    rows += [jnp.full((1, 128), NO_BLOCK, I32)] * (2 * index_rows - col_rows - 1) + [home_row]
    for r in range(index_rows):
        index[0, r : r + 1, :] = rows[r] + rows[index_rows + r] * WORD_HALF

    def index_row(start, size, r):
        word = index[start : start + size, r % index_rows, :]
        return word >> 16 if r >= index_rows else word & (WORD_HALF - 1)

    pl.semaphore_wait(barrier, devices - 1)
    for p in range(1, devices):
        pltpu.make_async_remote_copy(
            src_ref=index.at[0], dst_ref=index.at[back[p]],
            send_sem=index_send, recv_sem=index_recv.at[back[p] // group],
            device_id=device_at[p], device_id_type=MESH,
        ).start()

    row_slot = jnp.zeros((1, adm), I32)
    near_row = jnp.zeros((1, near_n), I32)
    near_col = jnp.zeros((1, near_n), I32)
    far_rows = far[0:1, :]
    for s in range(nb):
        row_slot = jnp.where(far_rows == home[s], s, row_slot)
        near_row = jnp.where(near_list[0:1, :] == home[s], s, near_row)
        near_col = jnp.where(near_list[1:2, :] == home[s], s, near_col)
    place = iota((cols2, adm), 0)
    slot_hot[...] = hot(over(place, 16) * 8 + within(place, 8) == far[2:3, :])
    row_hot = hot(row_slot == within(iota((2 * nb, adm), 0), nb))
    pick = dot_nt(slot_hot[...], row_hot)
    comp = within(over(iota((cols2, 2 * nb), 0), 8), 2)
    row_sel[...] = jnp.where(comp == over(iota((cols2, 2 * nb), 1), nb), pick, 0.0).astype(BF)
    pick_t = dot_nt(row_hot, slot_hot[...])
    comp_t = within(over(iota((2 * nb, cols2), 1), 8), 2)
    row_sel_t[...] = jnp.where(comp_t == over(iota((2 * nb, cols2), 0), nb), pick_t, 0.0).astype(BF)
    tri[...] = hot(iota((adm, adm), 0) < iota((adm, adm), 1))
    tri_t[...] = hot(iota((adm, adm), 0) > iota((adm, adm), 1))
    col_ids = jnp.concatenate([far_cols.astype(F32), jnp.zeros((7, adm), F32)], axis=0).T
    far_col[...] = jnp.broadcast_to(col_ids[:, 0:1].astype(I32), (adm, devices))

    near_place = iota((2 * near_n, near_n), 0)
    near_hot = hot(over(near_place, 16) * 8 + within(near_place, 8) == near_list[2:3, :])
    block_of = within(iota((2 * nb, near_n), 0), nb)
    near_pick = dot_nt(near_hot, hot(near_col == block_of))
    comp = within(over(iota((2 * near_n, 2 * nb), 0), 8), 2)
    near_cols[...] = jnp.where(
        comp == over(iota((2 * near_n, 2 * nb), 1), nb), near_pick, 0.0
    ).astype(BF)
    near_pick_t = dot_nt(hot(near_row == block_of), near_hot)
    comp_t = within(over(iota((2 * nb, 2 * near_n), 1), 8), 2)
    near_rows[...] = jnp.where(
        comp_t == over(iota((2 * nb, 2 * near_n), 0), nb), near_pick_t, 0.0
    ).astype(BF)

    rep_rows = devices * per
    rep[...] = hot(over(iota((group * per, group), 0), per) == iota((group * per, group), 1))

    def by_block(ref):
        whole = ref[...].astype(F32)
        for c in range(2):
            for s in range(nb):
                field[c * nb + s : c * nb + s + 1, :] = whole[c : c + 1, s * block : (s + 1) * block]
        return field[...]

    def by_patch(value, ref):
        field[...] = value
        for c in range(2):
            for s in range(nb):
                ref[c : c + 1, s * block : (s + 1) * block] = field[c * nb + s : c * nb + s + 1, :]

    def wait_bytes(ref, sem):
        pltpu.make_async_copy(ref, ref, sem).wait()

    diag = within(iota((16, 8 * rank), 0), 8) == over(iota((16, 8 * rank), 1), rank)
    unroll = 24 if tiles % 24 == 0 else 1

    def over_tiles(step):
        def body(i, carry):
            for k in range(unroll):
                step(i * unroll + k)
            return carry

        lax.fori_loop(0, tiles // unroll, body, 0)

    def contract(factor):
        def step(t):
            y = dot_nt(left[rows_at(t * 16, 16), :], factor[rows_at(t * 8 * rank, 8 * rank), :])
            mid[rows_at(t * 16, 16), :] = jnp.where(diag, y, 0.0).astype(BF)

        over_tiles(step)

    def expand(factor, split):
        def step(t):
            y = dot_nn(mid[rows_at(t * 16, 16), :], factor[rows_at(t * 8 * rank, 8 * rank), :])
            high = y.astype(BF)
            terms[rows_at(t * 16, 16), :] = high
            if split:
                terms_low[rows_at(t * 16, 16), :] = (y - high.astype(F32)).astype(BF)

        over_tiles(step)

    def send(n, p):
        pltpu.make_async_remote_copy(
            src_ref=sent.at[n, p], dst_ref=got.at[n, back[p]],
            send_sem=send_sem.at[n], recv_sem=recv_sem.at[n],
            device_id=device_at[p], device_id_type=MESH,
        ).start()

    def exchange(n, sel, right, order, later=False):
        left_over = []
        for i in order:
            y = dot_nn(sel[i * part * per : (i + 1) * part * per, :], right)
            y = y.reshape(part, per, block)
            y = jnp.concatenate([y[:, :, :half], y[:, :, half:]], axis=1)
            sent[n, i * part : (i + 1) * part] = y.astype(BF)
            for p in range((i + 1) * part - 1, i * part - 1, -1):
                if p == 0:
                    got[n, 0] = sent[n, 0]
                elif later:
                    left_over.append((n, p))
                else:
                    send(n, p)
        return left_over

    def send_share(waiting, done, steps):
        for n, p in waiting[len(waiting) * done // steps : len(waiting) * (done + 1) // steps]:
            send(n, p)

    parts = devices // part
    far_parts = range(parts - 1, -1, -1)

    def land(n):
        wait_bytes(got.at[n, pl.ds(0, devices - 1)], recv_sem.at[n])
        y = got[n].astype(F32)
        y = jnp.concatenate([y[:, :per, :], y[:, per:, :]], axis=2)
        flat[...] = y.reshape(rep_rows, block).astype(BF)

    def send_rates(n, x, order, later=False):
        return exchange(n, reply_sel, jnp.concatenate([x] * cap, axis=0), order, later)

    def near_part(x, waiting):
        near_left[...] = dot_nn(near_cols[...], x).astype(BF)
        which = within(iota((16, block), 0), 8)
        for t in range(near_n // 8):
            x_tile = near_left[t * 16 : (t + 1) * 16, :]
            y = jnp.zeros((16, block), F32)
            for j in range(8):
                g = t * 8 + j
                y = jnp.where(which == j, dot_nt(x_tile, near[g * block : (g + 1) * block, :]), y)
                send_share(waiting, g, near_n)
            high = y.astype(BF)
            near_high[t * 16 : (t + 1) * 16, :] = high
            near_low[t * 16 : (t + 1) * 16, :] = (y - high.astype(F32)).astype(BF)
        return dot_nn(near_rows[...], near_high[...]) + dot_nn(near_rows[...], near_low[...])

    def row_rates(x):
        left[...] = dot_nn(row_sel[...], x).astype(BF)

    def send_back(n):
        return exchange(n, col_sel_t, terms[...], far_parts, True)

    def finish(n_rates, n_back, total):
        land(n_rates)
        left[...] = dot_nn(col_sel[...], flat[...]).astype(BF)
        contract(v)
        expand(u, True)
        total = total + dot_nn(row_sel_t[...], terms[...])
        total = total + dot_nn(row_sel_t[...], terms_low[...])
        land(n_back)
        return total + dot_nn(reply_sel_t[...], flat[...])

    scale[...] = by_block(effect)
    x = by_block(slip).astype(BF)
    row_rates(x)
    loads[0].wait()
    contract(u)

    loads[1].wait()
    expand(v, False)

    lanes = 2 * nb * cap
    lane_k = over(iota((group, lanes), 1), 2 * nb)
    lane_s = within(iota((group, lanes), 1), nb) + 1
    reply_mask = within(iota((group * per, lanes), 0), per) == over(iota((group * per, lanes), 1), nb)
    for h in range(2):
        wait_bytes(index.at[pl.ds(0, group - 1 + h)], index_recv.at[h])
        first_of, end = h * group, (h + 1) * group
        for q in range(first_of, end, part):
            wanted = jnp.concatenate(
                [index_row(q, part, r) for r in range(col_rows)], axis=1
            )[:, :adm]
            val = jnp.zeros((part, adm), F32)
            for s in range(nb):
                val = jnp.where(wanted == home[s], float(s + 1), val)
            slot_val[q : q + part, :] = val
            pair_hot[q : q + part, :] = hot(val > 0.0)
        ranks = dot_nn(pair_hot[first_of:end, :], tri[...])
        chosen = jnp.zeros((group, lanes), F32)
        for k in range(cap):
            slot_k = jnp.sum(
                jnp.where(ranks == float(k), slot_val[first_of:end, :], 0.0), axis=1, keepdims=True
            )
            chosen = jnp.where(lane_k == k, slot_k, chosen)
        wants = jnp.where(chosen == lane_s.astype(F32), 1.0, 0.0)
        spread = dot_nn(rep[...], wants.astype(BF))
        reply_sel[first_of * per : end * per, :] = jnp.where(reply_mask, spread, 0.0).astype(BF)
        send_rates(0, x, range(h * parts // 2, (h + 1) * parts // 2))

    homes = index_row(0, devices, 2 * index_rows - 1).astype(F32).T.astype(I32)
    tall = 128 if adm % 128 == 0 else adm
    founds = []
    for q in range(0, adm, tall):
        ids = far_col[q : q + tall, :]
        found = jnp.zeros((tall, devices), F32)
        for s in range(nb):
            found = jnp.where(ids == homes[s : s + 1, :], 1.0, found)
        founds.append(found.astype(BF))
    found = jnp.concatenate(founds, axis=0)
    place_in = (dot_nn(tri_t[...], found) * found.astype(F32)).astype(BF)
    owner = dot_nt(iota((8, devices), 1).astype(BF), found)
    place_in = dot_nt(jnp.ones((8, devices), BF), place_in)
    both = jnp.concatenate([owner[0:1], place_in[0:1], jnp.zeros((6, adm), F32)], axis=0).astype(BF)
    to_row = dot_nt(both, slot_hot[...])
    to_row = (to_row[0:1] * per + to_row[1:2] * 2).astype(I32)
    to_row = to_row + within(over(iota((1, cols2), 1), 8), 2)
    band = min(128, rep_rows)

    def rows_body(i, carry):
        col_sel_t[rows_at(i * band, band), :] = hot(iota((band, cols2), 0) == to_row - i * band)
        return carry

    lax.fori_loop(0, rep_rows // band, rows_body, 0)
    waiting = send_back(1)
    loads[2].wait()
    near_sum = near_part(x, waiting)

    side = 256 if cols2 % 256 == 0 else cols2

    for i in range(0, rep_rows, band):
        for k in range(0, cols2, side):
            col_sel[k : k + side, i : i + band] = col_sel_t[i : i + band, k : k + side].T

    fold = hot(within(iota((2 * nb, lanes), 1), 2 * nb) == iota((2 * nb, lanes), 0))
    reply_sel_t[...] = dot_nt(fold, reply_sel[...]).astype(BF)

    first = finish(0, 1, near_sum)
    x = (x.astype(F32) * jnp.exp(jnp.tanh(first / scale[...]))).astype(BF)
    send_rates(2, x, far_parts)
    by_patch(first, first_out)
    first_copy = pltpu.make_async_copy(first_out, first_hbm, out_sem.at[0])
    first_copy.start()
    row_rates(x)
    contract(u)
    expand(v, False)
    waiting = send_back(3)
    by_patch(finish(2, 3, near_part(x, waiting)), second_out)
    second_copy = pltpu.make_async_copy(second_out, second_hbm, out_sem.at[1])
    second_copy.start()

    wait_bytes(index.at[pl.ds(0, devices - 1)], index_send)
    first_copy.wait()
    second_copy.wait()
    for n in range(4):
        wait_bytes(sent.at[n, pl.ds(0, devices - 1)], send_sem.at[n])


def hand_out(first_in, second_in, first_out, second_out):
    first_out[...] = first_in[...]
    second_out[...] = second_in[...]


def local(slip, effect_stress, home_blocks, far_list, u_factor, v_factor, near_list, near_block):
    wide_n, narrow_n = lax.axis_size("wide"), lax.axis_size("narrow")
    devices = wide_n * narrow_n
    nb = home_blocks.shape[0]
    block = slip.shape[1] // nb
    adm, rank, _ = u_factor.shape
    near_n = near_list.shape[1]
    cap = max(2, adm // devices + 1)
    per = 2 * cap
    rep_rows = devices * per
    cols2 = 2 * adm
    index_rows = (-(-adm // 128) + 2) // 2
    dims = (wide_n, narrow_n, nb, cap, adm, near_n, block, rank)
    vmem = pl.BlockSpec(memory_space=pltpu.VMEM)
    hbm = pl.BlockSpec(memory_space=pl.ANY)
    field = jax.ShapeDtypeStruct((2, nb * block), F32)
    dma = pltpu.SemaphoreType.DMA
    results = pl.pallas_call(
        functools.partial(kernel, dims),
        out_shape=(field, field),
        in_specs=[hbm] * 8,
        out_specs=(hbm, hbm),
        scratch_shapes=[
            pltpu.SMEM(home_blocks.shape, I32),
            pltpu.VMEM(far_list.shape, I32),
            pltpu.VMEM(near_list.shape, I32),
            pltpu.VMEM(slip.shape, BF),
            pltpu.VMEM(slip.shape, F32),
            pltpu.VMEM(slip.shape, F32),
            pltpu.VMEM(slip.shape, F32),
            pltpu.VMEM((adm * rank, block), BF),
            pltpu.VMEM((adm * rank, block), BF),
            pltpu.VMEM((near_n * block, block), BF),
            pltpu.VMEM((devices, index_rows, 128), I32),
            pltpu.VMEM((devices, adm), BF),
            pltpu.VMEM((devices, adm), F32),
            pltpu.VMEM((adm, adm), BF),
            pltpu.VMEM((adm, adm), BF),
            pltpu.VMEM((adm, devices), I32),
            pltpu.VMEM((cols2, adm), BF),
            pltpu.VMEM((cols2, 2 * nb), BF),
            pltpu.VMEM((2 * nb, cols2), BF),
            pltpu.VMEM((2 * near_n, 2 * nb), BF),
            pltpu.VMEM((2 * nb, 2 * near_n), BF),
            pltpu.VMEM((2 * near_n, block), BF),
            pltpu.VMEM((2 * near_n, block), BF),
            pltpu.VMEM((2 * near_n, block), BF),
            pltpu.VMEM((cols2, rep_rows), BF),
            pltpu.VMEM((rep_rows, cols2), BF),
            pltpu.VMEM((rep_rows, 2 * nb * cap), BF),
            pltpu.VMEM((2 * nb, rep_rows), BF),
            pltpu.VMEM((rep_rows // 2, devices // 2), BF),
            pltpu.VMEM((cols2, block), BF),
            pltpu.VMEM((cols2, 8 * rank), BF),
            pltpu.VMEM((cols2, block), BF),
            pltpu.VMEM((cols2, block), BF),
            pltpu.VMEM((rep_rows, block), BF),
            pltpu.VMEM((4, devices, 2 * per, block // 2), BF),
            pltpu.VMEM((4, devices, 2 * per, block // 2), BF),
            pltpu.VMEM((2 * nb, block), F32),
            pltpu.VMEM((2 * nb, block), F32),
            dma((5,)),
            dma((2,)),
            dma((3,)),
            dma(()),
            dma((2,)),
            dma((4,)),
            dma((4,)),
        ],
        compiler_params=pltpu.CompilerParams(
            collective_id=0, has_side_effects=True, vmem_limit_bytes=56 << 20
        ),
        name="stress_two_steps",
    )(
        home_blocks,
        far_list,
        near_list,
        slip,
        effect_stress,
        u_factor.reshape(adm * rank, block),
        v_factor.reshape(adm * rank, block),
        near_block.reshape(near_n * block, block),
    )
    return pl.pallas_call(
        hand_out,
        out_shape=(field, field),
        in_specs=[vmem, vmem],
        out_specs=(vmem, vmem),
        name="hand_out",
    )(*results)


def solution(mesh):
    in_specs = (
        P(None, AXES),
        P(None, AXES),
        P(AXES),
        P(None, AXES),
        P(AXES, None, None),
        P(AXES, None, None),
        P(None, AXES),
        P(AXES, None, None),
    )
    out_specs = (P(None, AXES), P(None, AXES))
    return jax.shard_map(local, mesh=mesh, in_specs=in_specs, out_specs=out_specs, check_vma=False)
```
